32 devices in a mesh: fsdp: 32 (over z, y, x, core).
Axes of the slice: x: 2, y: 2, z: 4, core: 2. Of those that a mesh axis runs over, the one named last changes fastest.
Arguments:
- tokens: bfloat16 [32768, 1024], P('fsdp'), may hold values from -6 to 6
- segments: int32 [32, 1024], P('fsdp'), may hold values from 0 to 7, never falling along the last dimension, each value on 1 to 512 neighbouring positions
- cotangent: bfloat16 [32768, 1024], P('fsdp'), may hold values from -6 to 6
- w_query: bfloat16 [1024, 2048], P('fsdp'), may hold values from -0.1875 to 0.1875
- w_key: bfloat16 [1024, 1024], P('fsdp'), may hold values from -0.1875 to 0.1875
- w_value: bfloat16 [1024, 1024], P('fsdp'), may hold values from -0.1875 to 0.1875
- w_out: bfloat16 [2048, 1024], P(None, 'fsdp'), may hold values from -1 to 1
- w_gate: bfloat16 [1024, 3072], P('fsdp'), may hold values from -0.1875 to 0.1875
- w_up: bfloat16 [1024, 3072], P('fsdp'), may hold values from -0.1875 to 0.1875
- w_down: bfloat16 [3072, 1024], P(None, 'fsdp'), may hold values from -0.109375 to 0.109375
- attn_gain: bfloat16 [1024], P('fsdp'), may hold values from 0.099609375 to 1.8984375
- mlp_gain: bfloat16 [1024], P('fsdp'), may hold values from 0.099609375 to 1.8984375
- q_gain: bfloat16 [128], replicated, may hold values from 0.099609375 to 1.8984375
- k_gain: bfloat16 [128], replicated, may hold values from 0.099609375 to 1.8984375
Outputs:
- result: bfloat16 [32768, 1024], P('fsdp')
- grad_tokens: bfloat16 [32768, 1024], P('fsdp')
- grad_query: float32 [1024, 2048], P('fsdp')
- grad_key: float32 [1024, 1024], P('fsdp')
- grad_value: float32 [1024, 1024], P('fsdp')
- grad_out: float32 [2048, 1024], P(None, 'fsdp')
- grad_gate: float32 [1024, 3072], P('fsdp')
- grad_up: float32 [1024, 3072], P('fsdp')
- grad_down: float32 [3072, 1024], P(None, 'fsdp')
- grad_attn_gain: float32 [1024], P('fsdp')
- grad_mlp_gain: float32 [1024], P('fsdp')
- grad_q_gain: float32 [128], replicated
- grad_k_gain: float32 [128], replicated
The draws below stay inside these ranges and needn't reach their ends.
Inputs may be any that keep to these rules, and one draw needn't show every extreme that they name: `segments`: document numbers never fall along a sequence; a document is 1 to 512 tokens long, and one in each sequence is exactly that long.
All inputs are finite; a program needn't handle non-finite values.
Results may differ from the reference program's by a relative error of at most 0.014.
Values may be sent and summed in bfloat16 or wider, within the bound.
No kernel may reach another device: no remote copies, remote signals or barrier semaphores. Data moves between devices by JAX's collectives and lax.ppermute only.
A program may use at most 320 MiB of HBM per device.

```python
import math
import jax
import jax.numpy as jnp
import numpy as np
from jax import lax

D = 1024
QUERY_HEADS = 16
KEY_VALUE_HEADS = 8
HEAD_SIZE = 128
FF = 3072
TOK_DEV = 1024
QW = 2048
KW = 1024
TOKENS = 32768
N_FSDP = 32


def strengthened(array, stream_key, source, target, parts, factor):
    owner, partner = [(jnp.arange(array.shape[axis_at]) // (array.shape[axis_at] // parts)).reshape([-1 if axis == axis_at else 1 for axis in range(array.ndim)]) for axis_at in (source, target)]
    chosen = jax.random.permutation(stream_key, parts)[partner]
    strong = (owner == chosen) | (owner == (partner + parts // 2) % parts)
    return jnp.where(strong, factor * array, array)


def block_scale(rng, dims, shards, smallest, high):
    level, own = 1.0, jax.random.fold_in(rng, 6)
    for dim, parts in shards:
        heights = jnp.exp(jax.random.uniform(jax.random.fold_in(own, dim), (parts,), jnp.float32, smallest / len(shards), high / len(shards)))
        level = level * jnp.repeat(heights, dims[dim] // parts).reshape([-1 if axis == dim else 1 for axis in range(len(dims))])
    return level


def length_profile(number_of, total, limit, slope):
    portions = [(1 << 20) // math.isqrt(grade ** slope) + 1 for grade in range(2, number_of + 1)]
    spare, given = total - limit - (number_of - 1), [1] * (number_of - 1)
    while spare > 0:
        free = [i for i in range(number_of - 1) if given[i] < limit]
        whole, remaining = sum([portions[i] for i in free]), spare
        for i in free:
            more = min(limit - given[i], max(1, remaining * portions[i] // whole), spare)
            given[i] = given[i] + more
            spare = spare - more
    return np.array([limit] + given)


def ragged_sizes(own_key, amount, total, reach, lean):
    if amount == 2:
        one = jax.random.randint(own_key, (), max(1, total - reach), min(reach, total - 1) + 1)
        return jnp.stack([one, total - one])
    sizes = jnp.asarray(length_profile(amount, total, reach, lean), jnp.int32)
    pairs = (amount - 1) // 2
    giver, receiver = sizes[1:1 + 2 * pairs:2], sizes[2:2 + 2 * pairs:2]
    room = jnp.minimum(giver - 1, reach - receiver)
    moved = jax.random.randint(jax.random.fold_in(own_key, 1), (pairs,), 0, 1 << 20) % (room + 1)
    sizes = sizes.at[1:1 + 2 * pairs:2].set(giver - moved).at[2:2 + 2 * pairs:2].set(receiver + moved)
    return sizes[jax.random.permutation(jax.random.fold_in(own_key, 2), amount)]


def centred(stream_key, dims, spread, most, cuts=(), kind=jnp.bfloat16):
    level = block_scale(stream_key, dims, cuts, -0.22, 0.18) if cuts else 1.0
    drawn = jax.random.normal(stream_key, dims, jnp.float32) * spread * level
    return jnp.minimum(jnp.maximum(drawn, -most), most).astype(kind)


def noise_with(own_key, extent, spread, bound, cuts, heavy, kind=jnp.bfloat16):
    values = spread * jax.random.normal(own_key, extent, jnp.float32)
    if cuts:
        values = values * block_scale(own_key, extent, cuts, -0.22, 0.18)
    return jnp.clip(strengthened(values, jax.random.fold_in(own_key, 3), *heavy), -bound, bound).astype(kind)


def setup_inputs(seed: int = 0) -> dict:
    streams_of = jax.random.split(jax.random.key(seed), 15)
    tokens = noise_with(streams_of[0], (TOKENS, D), 1.0, 6.0, ((0, 32),), (0, 1, 32, 2.75))
    segments = jax.vmap(lambda own: jnp.searchsorted(jnp.cumsum(ragged_sizes(own, max(TOK_DEV // 128, 4), TOK_DEV, TOK_DEV // 2, 1)), jnp.arange(TOK_DEV), side="right"))(jax.random.split(streams_of[1], N_FSDP)).reshape((N_FSDP, TOK_DEV)).astype(jnp.int32)
    cotangent = noise_with(streams_of[2], (TOKENS, D), 1.0, 6.0, ((0, 32),), (0, 1, 32, 2.75))
    w_query = centred(streams_of[3], (D, QW), D ** -0.5, 0.1875, ((0, 32),))
    w_key = centred(streams_of[4], (D, KW), D ** -0.5, 0.1875, ((0, 32),))
    w_value = centred(streams_of[5], (D, KW), D ** -0.5, 0.1875, ((0, 32),))
    w_out = centred(streams_of[6], (QW, D), (max(QW // 64, 1)) ** -0.5, 1.0, ((1, 32),))
    w_gate = centred(streams_of[7], (D, FF), D ** -0.5, 0.1875, ((0, 32),))
    w_up = centred(streams_of[8], (D, FF), D ** -0.5, 0.1875, ((0, 32),))
    w_down = centred(streams_of[9], (FF, D), FF ** -0.5, 0.109375, ((1, 32),))
    attn_gain = jnp.clip(1.0 + 0.18 * jax.random.normal(streams_of[10], (D,), jnp.float32), 0.099609375, 1.8984375).astype(jnp.bfloat16)
    mlp_gain = jnp.clip(1.0 + 0.18 * jax.random.normal(streams_of[11], (D,), jnp.float32), 0.099609375, 1.8984375).astype(jnp.bfloat16)
    q_gain = jnp.clip(1.0 + 0.18 * jax.random.normal(streams_of[12], (HEAD_SIZE,), jnp.float32), 0.099609375, 1.8984375).astype(jnp.bfloat16)
    k_gain = jnp.clip(1.0 + 0.18 * jax.random.normal(streams_of[13], (HEAD_SIZE,), jnp.float32), 0.099609375, 1.8984375).astype(jnp.bfloat16)
    return {"tokens": tokens, "segments": segments, "cotangent": cotangent, "w_query": w_query, "w_key": w_key, "w_value": w_value, "w_out": w_out, "w_gate": w_gate, "w_up": w_up, "w_down": w_down, "attn_gain": attn_gain, "mlp_gain": mlp_gain, "q_gain": q_gain, "k_gain": k_gain}


@jax.custom_vjp
def narrow_precision(v):
    return lax.optimization_barrier(v.astype(jnp.bfloat16)).astype(jnp.float32)

@jax.custom_vjp
def narrow_backward(v):
    return v

def low_keep(v):
    return (narrow_precision(v), None)

def low_pass(kept, grad):
    return (grad,)

def back_keep(v):
    return (v, None)

def back_low(kept, grad):
    return (narrow_precision(grad),)
narrow_precision.defvjp(low_keep, low_pass)
narrow_backward.defvjp(back_keep, back_low)
EPS = 1e-06
THETA = 1000000.0
HIGH = lax.Precision.HIGHEST

def matrix_product(left, right):
    return jnp.dot(left, right, precision=HIGH)

def root_mean_square_norm(value_rows, gain):
    return value_rows * lax.rsqrt(lax.optimization_barrier(jnp.mean(value_rows * value_rows, axis=-1, keepdims=True)) + EPS) * gain

def places(segment_row):
    index = jnp.arange(segment_row.shape[0], dtype=jnp.int32)
    previous = jnp.concatenate([segment_row[:1] - 1, segment_row[:-1]])
    starts = jnp.where(segment_row != previous, index, 0)
    return index - lax.cummax(starts, axis=0)

def rotary_embed(value_rows, select_positions):
    half = value_rows.shape[-1] // 2
    freq = THETA ** (-jnp.arange(half, dtype=jnp.float32) / half)
    turned = select_positions.astype(jnp.float32)[:, None] * freq[None, :]
    rotary_cosine = jnp.cos(turned)[:, None, :]
    rotary_sine = jnp.sin(turned)[:, None, :]
    first = value_rows[..., :half]
    second = value_rows[..., half:]
    return jnp.concatenate([first * rotary_cosine - second * rotary_sine, second * rotary_cosine + first * rotary_sine], axis=-1)

def layer(inputs, segment_row, wq, key_matrix, value_matrix, wo, wg, wu, wd, gain_a, gain_m, query_norm_scale, key_norm_scale):
    token_rows = inputs.shape[0]
    index = jnp.arange(token_rows, dtype=jnp.int32)
    select_positions = places(segment_row)
    first_normalized1 = narrow_precision(root_mean_square_norm(inputs, gain_a))
    query_unnormalized = narrow_backward(matrix_product(first_normalized1, wq)).reshape(token_rows, QUERY_HEADS, HEAD_SIZE)
    key_unnormalized = narrow_backward(matrix_product(first_normalized1, key_matrix)).reshape(token_rows, KEY_VALUE_HEADS, HEAD_SIZE)
    value_rows = narrow_precision(narrow_backward(matrix_product(first_normalized1, value_matrix))).reshape(token_rows, KEY_VALUE_HEADS, HEAD_SIZE)
    query_rows = narrow_precision(rotary_embed(root_mean_square_norm(query_unnormalized, query_norm_scale), select_positions)).reshape(token_rows, KEY_VALUE_HEADS, QUERY_HEADS // KEY_VALUE_HEADS, HEAD_SIZE)
    keys = narrow_precision(rotary_embed(root_mean_square_norm(key_unnormalized, key_norm_scale), select_positions))
    scores = narrow_backward(jnp.einsum('qgrd,kgd->grqk', query_rows, keys, precision=HIGH) / math.sqrt(HEAD_SIZE))
    allowed = (segment_row[:, None] == segment_row[None, :]) & (index[:, None] >= index[None, :])
    scores = jnp.where(allowed, scores, -1e+30)
    top = lax.optimization_barrier(jnp.max(scores, axis=-1, keepdims=True))
    expo = jnp.exp(scores - top)
    probs = narrow_precision(expo / lax.optimization_barrier(jnp.sum(expo, axis=-1, keepdims=True)))
    mixed = jnp.einsum('grqk,kgd->qgrd', probs, value_rows, precision=HIGH).reshape(token_rows, QUERY_HEADS * HEAD_SIZE)
    mixed = narrow_precision(narrow_backward(mixed))
    after = inputs + narrow_backward(matrix_product(mixed, wo))
    normed2 = narrow_precision(root_mean_square_norm(after, gain_m))
    gate = narrow_backward(matrix_product(normed2, wg))
    up = narrow_backward(matrix_product(normed2, wu))
    hidden = narrow_precision(jax.nn.silu(gate) * up)
    return after + narrow_backward(matrix_product(hidden, wd))

def reference(tokens, segments, cotangent, w_query, w_key, w_value, w_out, w_gate, w_up, w_down, attn_gain, mlp_gain, q_gain, k_gain):
    weights = tuple((w.astype(jnp.float32) for w in (w_query, w_key, w_value, w_out, w_gate, w_up, w_down, attn_gain, mlp_gain, q_gain, k_gain)))
    inputs = tokens.astype(jnp.float32).reshape(N_FSDP, TOK_DEV, D)
    step_fn = jax.checkpoint(layer)

    def forward(inputs, weights):

        def one(carry, item):
            return (carry, step_fn(item[0], item[1], *weights))
        _, outputs = lax.scan(one, jnp.zeros((), jnp.float32), (inputs, segments))
        return outputs
    outputs, pull = jax.vjp(forward, inputs, weights)
    grad_in, grads = pull(cotangent.astype(jnp.float32).reshape(N_FSDP, TOK_DEV, D))
    return (outputs.reshape(TOKENS, D).astype(jnp.bfloat16), grad_in.reshape(TOKENS, D).astype(jnp.bfloat16), grads[0], grads[1], grads[2], grads[3], grads[4], grads[5], grads[6], grads[7], grads[8], grads[9], grads[10])
```

```python
import functools
import math

import jax
import jax.numpy as jnp
from jax import lax
from jax.experimental import pallas as pl
from jax.experimental.pallas import tpu as pltpu
from jax.sharding import PartitionSpec as P

AX = "fsdp"
D = 1024
HALF = D // 2
QUERY_HEADS = 16
KEY_VALUE_HEADS = 8
HEAD_SIZE = 128
FF = 3072
PART = FF // 2
GROUP = QUERY_HEADS // KEY_VALUE_HEADS
QW = QUERY_HEADS * HEAD_SIZE
KW = KEY_VALUE_HEADS * HEAD_SIZE
LONGEST = 512
BLK = 256
COLS = 512
EPS = 1e-06
THETA = 1000000.0
ROOT = math.sqrt(HEAD_SIZE)
SCALE2 = math.log2(math.e) / ROOT
VMEM = 56 * 1024 * 1024
F32 = jnp.float32
B16 = jnp.bfloat16


def axes_of(n):
    out, stride = [(1, 2)], 2
    for radix in (2, 2, 4, 4, 4, 4):
        if stride * radix <= n:
            out.append((stride, radix))
            stride *= radix
    while stride < n:
        out.append((stride, 2))
        stride *= 2
    return out


def move(value, n, axis, k):
    s, r = axis
    pairs = [(i, i + ((i // s % r + k) % r - i // s % r) * s) for i in range(n)]
    return lax.ppermute(value, AX, pairs)


def orders(n):
    m = len(axes_of(n)) - 1
    if m == 3:
        return [(2, 0, 1), (2, 1, 0), (0, 2, 1), (1, 2, 0)]
    return [tuple(range(m))[::-1]] * 4


def gather(value, n, order):
    ax = axes_of(n)[1:]
    rows, cols = value.shape
    value = value.reshape((1,) * len(ax) + value.shape)
    for a in order:
        cur, got = value, [value]
        for _ in range(ax[a][1] - 1):
            cur = move(cur, n, ax[a], -1)
            got.append(cur)
        value = jnp.concatenate(got, axis=a)
    value = value.reshape(rows * n // 2, cols)
    return value, move(value, n, (1, 2), 1)


def scatter(keep, give, n, order):
    ax = axes_of(n)[1:]
    rows, cols = keep.shape
    acc = keep.astype(F32) + move(give, n, (1, 2), 1).astype(F32)
    acc = acc.astype(B16).reshape(tuple(r for _, r in ax) + (rows * 2 // n, cols))
    for place, a in enumerate(order):
        r = ax[a][1]
        run = lax.index_in_dim(acc, r - 1, a, keepdims=True)
        for j in range(r - 2, -1, -1):
            mine = lax.index_in_dim(acc, j, a, keepdims=True).astype(F32)
            run = move(run, n, ax[a], 1).astype(F32) + mine
            if j > 0 or place < len(order) - 1:
                run = run.astype(B16)
        acc = run
    return acc.reshape(rows * 2 // n, cols)


def absolute_rows(n):
    ax = axes_of(n)
    me = lax.axis_index(AX)
    share = D // n
    place = lax.broadcasted_iota(jnp.int32, (D,), 0)
    rem = place // share
    owner = jnp.zeros_like(place)
    for s, r in ax[:0:-1]:
        owner = owner + ((me // s + rem % r) % r) * s
        rem = rem // r
    owner = owner + (me + rem) % 2
    return owner * share + place % share


def sum_all(value, n):
    step = 1
    while step < n:
        value = value + lax.ppermute(value, AX, [(i, i ^ step) for i in range(n)])
        step *= 2
    return value


def call(kernel, grid, ins, outs, shapes, scratch=(), flops=0, moved=0, name=None):
    return pl.pallas_call(
        kernel,
        grid=grid,
        in_specs=ins,
        out_specs=outs,
        out_shape=shapes,
        scratch_shapes=list(scratch),
        compiler_params=pltpu.CompilerParams(vmem_limit_bytes=VMEM),
        cost_estimate=pl.CostEstimate(flops=flops, bytes_accessed=moved, transcendentals=0),
        name=name,
    )


def whole(shape):
    return pl.BlockSpec(shape, lambda *_: (0,) * len(shape))


def rows_of(cols, blk=BLK):
    return pl.BlockSpec((blk, cols), lambda i: (i, 0))


def sds(shape, dtype):
    return jax.ShapeDtypeStruct(shape, dtype)


def nn(a, b):
    return lax.dot_general(a, b, (((1,), (0,)), ((), ())), preferred_element_type=F32)


def nt(a, b):
    return lax.dot_general(a, b, (((1,), (1,)), ((), ())), preferred_element_type=F32)


def inv_rms(x):
    return lax.rsqrt(jnp.mean(x * x, axis=-1, keepdims=True) + EPS)


def prep_kernel(tok, cot, perm, gain, trel, crel, n1):
    t = nn(tok[...], perm[...])
    trel[...] = t.astype(B16)
    n1[...] = (t * inv_rms(t) * gain[...]).astype(B16)
    crel[...] = nn(cot[...], perm[...]).astype(B16)


def prep(tokens, cotangent, perm, gain):
    t = tokens.shape[0]
    return call(
        prep_kernel,
        (t // BLK,),
        [rows_of(D), rows_of(D), whole((D, D)), whole((1, D))],
        [rows_of(D)] * 3,
        [sds((t, D), B16)] * 3,
        flops=4 * t * D * D,
        moved=12 * t * D,
        name="prep",
    )(tokens, cotangent, perm, gain)


def project_kernel(n1, wa, wb, cos, sin, gain, out, raw):
    for i in range(n1.shape[0] // BLK):
        at = pl.ds(i * BLK, BLK)
        x = nn(n1[at, :HALF], wa[...]) + nn(n1[at, HALF:], wb[...])
        raw[at, :] = x.astype(B16)
        for h in range(COLS // HEAD_SIZE):
            lanes = slice(h * HEAD_SIZE, (h + 1) * HEAD_SIZE)
            y = x[:, lanes]
            y = y * inv_rms(y) * gain[...]
            y = y * cos[at, :] + pltpu.roll(y, HEAD_SIZE // 2, 1) * sin[at, :]
            out[at, lanes] = y.astype(B16)


def project(n1, w, cos, sin, gain):
    t, cols = n1.shape[0], w[0].shape[1]
    wide = pl.BlockSpec((HALF, COLS), lambda j: (0, j))
    tall = pl.BlockSpec((t, COLS), lambda j: (0, j))
    return call(
        project_kernel,
        (cols // COLS,),
        [whole((t, D)), wide, wide, whole((t, HEAD_SIZE)), whole((t, HEAD_SIZE)), whole((1, HEAD_SIZE))],
        [tall, tall],
        [sds((t, cols), B16)] * 2,
        flops=2 * t * D * cols,
        moved=2 * (t * D + D * cols + 2 * t * cols),
        name="project",
    )(n1, *w, cos, sin, gain)


def plain_kernel(n1, wa, wb, out):
    out[...] = (nn(n1[:, :HALF], wa[...]) + nn(n1[:, HALF:], wb[...])).astype(B16)


def project_plain(n1, w):
    t, cols = n1.shape[0], w[0].shape[1]
    wide = pl.BlockSpec((HALF, COLS), lambda j: (0, j))
    return call(
        plain_kernel,
        (cols // COLS,),
        [whole((t, D)), wide, wide],
        pl.BlockSpec((t, COLS), lambda j: (0, j)),
        sds((t, cols), B16),
        flops=2 * t * D * cols,
        moved=2 * (t * D + D * cols + t * cols),
        name="project_plain",
    )(n1, *w)


def build_bias(first, bias):
    t = bias.shape[0]
    for i in range(t // BLK):
        at = slice(i * BLK, (i + 1) * BLK)
        key = lax.broadcasted_iota(jnp.int32, (t, BLK), 0)
        query = lax.broadcasted_iota(jnp.int32, (t, BLK), 1) + i * BLK
        allowed = (key >= first[:, at]) & (key <= query)
        bias[:, at] = jnp.where(allowed, 0.0, -1e30)


def window(i):
    return slice(max(0, i - LONGEST // BLK) * BLK, (i + 1) * BLK)


def stacked(ref, at):
    return jnp.concatenate([ref[at, :HEAD_SIZE], ref[at, HEAD_SIZE:]], axis=0)


def attend_kernel(q, k, v, first, out, lse, bias):
    @pl.when(pl.program_id(0) == 0)
    def _():
        build_bias(first, bias)

    vt = v[...].T
    for i in range(q.shape[0] // BLK):
        at = slice(i * BLK, (i + 1) * BLK)
        keys = window(i)
        s = nt(k[keys, :], stacked(q, at))
        b = bias[keys, at]
        e = jnp.exp2(s * SCALE2 + jnp.concatenate([b, b], axis=1))
        total = jnp.sum(e, axis=0, keepdims=True)
        o = (nn(vt[:, keys], e.astype(B16)) * (1.0 / total)).T.astype(B16)
        level = jnp.log2(total)
        for r in range(GROUP):
            mine = slice(r * BLK, (r + 1) * BLK)
            out[at, r * HEAD_SIZE : (r + 1) * HEAD_SIZE] = o[mine, :]
            lse[0, r : r + 1, at] = level[:, mine]


def attend(q, k, v, first):
    t = k.shape[0]
    pair = GROUP * HEAD_SIZE
    groups = k.shape[1] // HEAD_SIZE
    head = pl.BlockSpec((t, HEAD_SIZE), lambda g: (0, g))
    both = pl.BlockSpec((t, pair), lambda g: (0, g))
    return call(
        attend_kernel,
        (groups,),
        [both, head, head, whole((1, t))],
        [both, pl.BlockSpec((1, GROUP, t), lambda g: (g, 0, 0))],
        [sds((t, groups * pair), B16), sds((groups, GROUP, t), F32)],
        [pltpu.VMEM((t, t), F32)],
        flops=8 * groups * t * t * pair,
        moved=12 * t * groups * HEAD_SIZE,
        name="attend",
    )(q, k, v, first)


def after_kernel(o, wa, wb, trel, gain, x1, n2):
    x = jnp.concatenate([nt(o[...], wa[...]), nt(o[...], wb[...])], axis=1)
    x = x + trel[...].astype(F32)
    x1[...] = x
    n2[...] = (x * inv_rms(x) * gain[...]).astype(B16)


def after_attention(o, w, trel, gain):
    t = o.shape[0]
    return call(
        after_kernel,
        (t // BLK,),
        [rows_of(QW), whole((HALF, QW)), whole((HALF, QW)), rows_of(D), whole((1, D))],
        [rows_of(D), rows_of(D)],
        [sds((t, D), F32), sds((t, D), B16)],
        flops=2 * t * D * QW,
        moved=2 * (t * QW + D * QW + 4 * t * D),
        name="after_attention",
    )(o, *w, trel, gain)


def mlp_kernel(n2, c, ga, gb, ua, ub, da, db, hidden, dgate, dup):
    for i in range(n2.shape[0] // BLK):
        at = slice(i * BLK, (i + 1) * BLK)
        n_a, n_b = n2[at, :HALF], n2[at, HALF:]
        gate = nn(n_a, ga[...]) + nn(n_b, gb[...])
        up = nn(n_a, ua[...]) + nn(n_b, ub[...])
        dh = nn(c[at, :HALF], da[...]) + nn(c[at, HALF:], db[...])
        sig = jax.nn.sigmoid(gate)
        silu = gate * sig
        hidden[at, :] = (silu * up).astype(B16)
        dgate[at, :] = (dh * up * sig * (1.0 + gate * (1.0 - sig))).astype(B16)
        dup[at, :] = (dh * silu).astype(B16)


def mlp(n2, c, wg, wu, wd):
    t, cols = n2.shape[0], wg[0].shape[1]
    wide = pl.BlockSpec((HALF, COLS), lambda j: (0, j))
    return call(
        mlp_kernel,
        (cols // COLS,),
        [whole((t, D))] * 2 + [wide] * 6,
        [pl.BlockSpec((t, COLS), lambda j: (0, j))] * 3,
        [sds((t, cols), B16)] * 3,
        flops=6 * t * D * cols,
        moved=2 * (2 * t * D + 3 * D * cols + 3 * t * cols),
        name="mlp",
    )(n2, c, *wg, *wu, *wd)


def result_kernel(x1, perm, *refs):
    *pairs, out = refs
    lower, upper = x1[:, :HALF], x1[:, HALF:]
    for i in range(0, len(pairs), 3):
        h, wa, wb = pairs[i : i + 3]
        lower = lower + nt(h[...], wa[...])
        upper = upper + nt(h[...], wb[...])
    x = jnp.concatenate([lower, upper], axis=1).astype(B16)
    out[...] = nt(x, perm[...]).astype(B16)


def make_result(x1, perm, terms):
    t = x1.shape[0]
    specs, args = [], []
    for h, w in terms:
        specs += [rows_of(h.shape[1]), whole(w[0].shape), whole(w[1].shape)]
        args += [h, *w]
    return call(
        result_kernel,
        (t // BLK,),
        [rows_of(D), whole((D, D))] + specs,
        rows_of(D),
        sds((t, D), B16),
        flops=2 * t * D * (FF + D),
        moved=2 * (t * FF + D * FF + 3 * t * D + D * D),
        name="result",
    )(x1, perm, *args)


def mlp_back_kernel(x1, crel, gain, *refs):
    *pairs, dx1, datt = refs
    lower = upper = 0.0
    for i in range(0, len(pairs), 3):
        h, wa, wb = pairs[i : i + 3]
        lower = lower + nt(h[...], wa[...])
        upper = upper + nt(h[...], wb[...])
    x = x1[...]
    s = inv_rms(x)
    r = x * s
    grad = jnp.concatenate([lower, upper], axis=1) * gain[...]
    inner = jnp.mean(grad * r, axis=-1, keepdims=True)
    d = crel[...].astype(F32) + s * (grad - r * inner)
    dx1[...] = d
    datt[...] = d.astype(B16)


def mlp_back(x1, crel, gain, terms):
    t = x1.shape[0]
    specs, args = [], []
    for h, w in terms:
        specs += [rows_of(h.shape[1]), whole(w[0].shape), whole(w[1].shape)]
        args += [h, *w]
    return call(
        mlp_back_kernel,
        (t // BLK,),
        [rows_of(D), rows_of(D), whole((1, D))] + specs,
        [rows_of(D), rows_of(D)],
        [sds((t, D), F32), sds((t, D), B16)],
        flops=4 * t * D * FF,
        moved=4 * (t * FF + D * FF + 3 * t * D),
        name="mlp_back",
    )(x1, crel, gain, *args)


def head_back(dy, raw, cos, sin, gain):
    dn = dy * cos - pltpu.roll(dy, HEAD_SIZE // 2, 1) * sin
    x = raw.astype(F32)
    s = inv_rms(x)
    r = x * s
    grad = dn * gain
    inner = jnp.mean(grad * r, axis=-1, keepdims=True)
    return (s * (grad - r * inner)).astype(B16), jnp.sum(dn * r, axis=0, keepdims=True)


def attend_back_kernel(
    datt, wa, wb, q, k, v, rawq, rawk, lse, first, cos, sin, qgain, kgain,
    dq, dk, dv, gains, bias, do, dk_sum, dv_sum,
):
    @pl.when(pl.program_id(0) == 0)
    def _():
        build_bias(first, bias)
        gains[...] = jnp.zeros_like(gains)

    t = q.shape[0]
    for i in range(t // BLK):
        at = slice(i * BLK, (i + 1) * BLK)
        do[at, :] = (nn(datt[at, :HALF], wa[...]) + nn(datt[at, HALF:], wb[...])).astype(B16)
    kt = k[...].T
    dk_sum[...] = jnp.zeros_like(dk_sum)
    dv_sum[...] = jnp.zeros_like(dv_sum)
    for i in range(t // BLK):
        at = slice(i * BLK, (i + 1) * BLK)
        keys = window(i)
        q2, do2 = stacked(q, at), stacked(do, at)
        b = bias[keys, at]
        level = jnp.concatenate([lse[0, r : r + 1, at] for r in range(GROUP)], axis=1)
        s = nt(k[keys, :], q2)
        p = jnp.exp2(s * SCALE2 + jnp.concatenate([b, b], axis=1) - level)
        dp = nt(v[keys, :], do2)
        delta = jnp.sum(dp * p, axis=0, keepdims=True)
        ds = (p * (dp - delta)).astype(B16)
        dv_sum[keys, :] += nn(p.astype(B16), do2)
        dk_sum[keys, :] += nn(ds, q2)
        dq2 = nn(kt[:, keys], ds).T * (1.0 / ROOT)
        for r in range(GROUP):
            lanes = slice(r * HEAD_SIZE, (r + 1) * HEAD_SIZE)
            low, part = head_back(
                dq2[r * BLK : (r + 1) * BLK, :], rawq[at, lanes], cos[at, :], sin[at, :], qgain[...]
            )
            dq[at, lanes] = low
            gains[0:1, :] += part
    for i in range(t // BLK):
        at = slice(i * BLK, (i + 1) * BLK)
        low, part = head_back(
            dk_sum[at, :] * (1.0 / ROOT), rawk[at, :], cos[at, :], sin[at, :], kgain[...]
        )
        dk[at, :] = low
        gains[1:2, :] += part
    dv[...] = dv_sum[...].astype(B16)


def attend_back(datt, w, q, k, v, rawq, rawk, lse, first, cos, sin, qgain, kgain):
    t = k.shape[0]
    pair = GROUP * HEAD_SIZE
    groups = k.shape[1] // HEAD_SIZE
    head = pl.BlockSpec((t, HEAD_SIZE), lambda g: (0, g))
    both = pl.BlockSpec((t, pair), lambda g: (0, g))
    wide = pl.BlockSpec((HALF, pair), lambda g: (0, g))
    table = whole((t, HEAD_SIZE))
    gain = whole((1, HEAD_SIZE))
    return call(
        attend_back_kernel,
        (groups,),
        [whole((t, D)), wide, wide, both, head, head, both, head,
         pl.BlockSpec((1, GROUP, t), lambda g: (g, 0, 0)), whole((1, t)), table, table, gain, gain],
        [both, head, head, whole((8, HEAD_SIZE))],
        [sds((t, groups * pair), B16), sds((t, groups * HEAD_SIZE), B16),
         sds((t, groups * HEAD_SIZE), B16), sds((8, HEAD_SIZE), F32)],
        [pltpu.VMEM((t, t), F32), pltpu.VMEM((t, pair), B16),
         pltpu.VMEM((t, HEAD_SIZE), F32), pltpu.VMEM((t, HEAD_SIZE), F32)],
        flops=2 * t * D * groups * pair + 10 * groups * t * t * pair,
        moved=2 * (t * D + D * groups * pair) + 24 * t * groups * HEAD_SIZE,
        name="attend_back",
    )(datt, *w, q, k, v, rawq, rawk, lse, first, cos, sin, qgain, kgain)


def weight_grad_kernel(x, g, out, xt):
    @pl.when(pl.program_id(0) == 0)
    def _():
        xt[...] = x[...].T

    out[...] = nn(xt[...], g[...]).astype(B16)


def weight_grad(x, half, g, col0=0, cols=None):
    t = x.shape[0]
    cols = g.shape[1] if cols is None else cols
    return call(
        weight_grad_kernel,
        (cols // COLS,),
        [pl.BlockSpec((t, HALF), lambda j: (0, half)),
         pl.BlockSpec((t, COLS), lambda j: (0, j + col0 // COLS))],
        pl.BlockSpec((HALF, COLS), lambda j: (0, j)),
        sds((HALF, cols), B16),
        [pltpu.VMEM((HALF, t), B16)],
        flops=2 * t * HALF * cols,
        moved=2 * (t * HALF + t * cols + HALF * cols),
        name="weight_grad",
    )(x, g)


def input_back_kernel(trel, dx1, gain, perm, *refs):
    *pairs, out = refs
    lower = upper = 0.0
    for i in range(0, len(pairs), 3):
        h, wa, wb = pairs[i : i + 3]
        lower = lower + nt(h[...], wa[...])
        upper = upper + nt(h[...], wb[...])
    x = trel[...].astype(F32)
    s = inv_rms(x)
    r = x * s
    grad = jnp.concatenate([lower, upper], axis=1) * gain[...]
    inner = jnp.mean(grad * r, axis=-1, keepdims=True)
    d = (dx1[...] + s * (grad - r * inner)).astype(B16)
    out[...] = nt(d, perm[...]).astype(B16)


def input_back(trel, dx1, gain, perm, terms):
    t = trel.shape[0]
    specs, args = [], []
    for h, at, w in terms:
        cols = w[0].shape[1]
        specs += [pl.BlockSpec((BLK, cols), lambda i, at=at: (i, at)), whole(w[0].shape), whole(w[1].shape)]
        args += [h, *w]
    return call(
        input_back_kernel,
        (t // BLK,),
        [rows_of(D), rows_of(D), whole((1, D)), whole((D, D))] + specs,
        rows_of(D),
        sds((t, D), B16),
        flops=2 * t * D * (QW + 2 * KW + D),
        moved=2 * (t * (QW + 2 * KW) + D * (QW + 2 * KW) + 4 * t * D + D * D),
        name="input_back",
    )(trel, dx1, gain, perm, *args)


def run_starts(segment_row):
    index = jnp.arange(segment_row.shape[0], dtype=jnp.int32)
    previous = jnp.concatenate([segment_row[:1] - 1, segment_row[:-1]])
    return index, lax.cummax(jnp.where(segment_row != previous, index, 0), axis=0)


def per_device(
    n, tokens, segments, cotangent, w_query, w_key, w_value, w_out, w_gate, w_up, w_down,
    attn_gain, mlp_gain, q_gain, k_gain,
):
    share = D // n
    od = orders(n)
    both = jnp.concatenate([attn_gain, mlp_gain]).reshape(1, 2 * share)
    ga, gb = gather(both, n, od[0])
    gains = jnp.concatenate([ga, gb], axis=0).astype(F32)
    gain_a = gains[:, :share].reshape(1, D)
    gain_m = gains[:, share:].reshape(1, D)
    wq = [gather(w_query[:, :KW], n, od[0]), gather(w_query[:, KW:], n, od[1])]
    wk = gather(w_key, n, od[2])
    wv = gather(w_value, n, od[3])
    out_t, down_t = w_out.T, w_down.T
    wo = gather(out_t, n, od[0])
    wg, wu, wd = [], [], []
    for i in range(2):
        cols = slice(i * PART, (i + 1) * PART)
        wg.append(gather(w_gate[:, cols], n, od[(1 + i) % 4]))
        wu.append(gather(w_up[:, cols], n, od[(2 + i) % 4]))
        wd.append(gather(down_t[:, cols], n, od[(3 + i) % 4]))

    index, first = run_starts(segments[0])
    half = HEAD_SIZE // 2
    freq = THETA ** (-jnp.arange(half, dtype=F32) / half)
    turned = (index - first).astype(F32)[:, None] * freq[None, :]
    cos, sin = jnp.cos(turned), jnp.sin(turned)
    cos = jnp.concatenate([cos, cos], axis=1)
    sin = jnp.concatenate([-sin, sin], axis=1)
    first = first.reshape(1, -1)
    qg = q_gain.astype(F32).reshape(1, HEAD_SIZE)
    kg = k_gain.astype(F32).reshape(1, HEAD_SIZE)
    perm = (jnp.arange(D, dtype=jnp.int32)[:, None] == absolute_rows(n)[None, :]).astype(B16)

    trel, crel, n1 = prep(tokens, cotangent, perm, gain_a)
    q0, rawq0 = project(n1, wq[0], cos, sin, qg)
    q1, rawq1 = project(n1, wq[1], cos, sin, qg)
    k, rawk = project(n1, wk, cos, sin, kg)
    v = project_plain(n1, wv)
    q = jnp.concatenate([q0, q1], axis=1)
    rawq = jnp.concatenate([rawq0, rawq1], axis=1)
    o, lse = attend(q, k, v, first)
    x1, n2 = after_attention(o, wo, trel, gain_m)

    acts = [mlp(n2, crel, wg[i], wu[i], wd[i]) for i in range(2)]
    sums = {}

    def send(key, x, g, order, col0=0, cols=None):
        give = weight_grad(x, 1, g, col0, cols)
        keep = weight_grad(x, 0, g, col0, cols)
        sums[key] = scatter(keep, give, n, od[order][::-1])

    for i, (hidden, dgate, dup) in enumerate(acts):
        send(("down", i), crel, hidden, 2 * i)
        send(("gate", i), n2, dgate, 2 * i + 1)
        send(("up", i), n2, dup, 2 - 2 * i)
    dx1, datt = mlp_back(
        x1, crel, gain_m, [(a[1], w) for a, w in zip(acts, wg)] + [(a[2], w) for a, w in zip(acts, wu)]
    )
    send("out", datt, o, 3)
    dq, dk, dv, head_gains = attend_back(
        datt, wo, q, k, v, rawq, rawk, lse, first, cos, sin, qg, kg
    )
    send(("q", 0), n1, dq, 0, 0, KW)
    send(("q", 1), n1, dq, 1, KW, KW)
    send("k", n1, dk, 2)
    send("v", n1, dv, 3)
    head_gains = sum_all(head_gains, n)
    grad_tokens = input_back(
        trel, dx1, gain_a, perm, [(dq, 0, wq[0]), (dq, 1, wq[1]), (dk, 0, wk), (dv, 0, wv)]
    )
    result = make_result(x1, perm, [(a[0], w) for a, w in zip(acts, wd)])

    grad_query = jnp.concatenate([sums["q", 0], sums["q", 1]], axis=1)
    grad_gate, grad_up, grad_down = [
        jnp.concatenate([sums[key, 0], sums[key, 1]], axis=1) for key in ("gate", "up", "down")
    ]

    def gain_grad(gain, *pairs):
        return sum(jnp.sum(w.astype(F32) * g, axis=1) for w, g in pairs) / gain.astype(F32)

    return (
        result,
        grad_tokens,
        grad_query,
        sums["k"],
        sums["v"],
        sums["out"].T,
        grad_gate,
        grad_up,
        grad_down.T,
        gain_grad(attn_gain, (w_query, grad_query), (w_key, sums["k"]), (w_value, sums["v"])),
        gain_grad(mlp_gain, (w_gate, grad_gate), (w_up, grad_up)),
        head_gains[0],
        head_gains[1],
    )


def solution(mesh):
    n = mesh.shape[AX]
    rows, cols, one = P(AX, None), P(None, AX), P(AX)
    in_specs = (rows, rows, rows, rows, rows, rows, cols, rows, rows, cols, one, one, P(), P())
    out_specs = (rows, rows, rows, rows, rows, cols, rows, rows, cols, one, one, P(), P())
    return jax.shard_map(
        functools.partial(per_device, n), mesh=mesh, in_specs=in_specs, out_specs=out_specs, check_vma=False
    )
```

```python
import functools
import math

import jax
import jax.numpy as jnp
from jax import lax
from jax.experimental import pallas as pl
from jax.experimental.pallas import tpu as pltpu
from jax.sharding import PartitionSpec as P

AX = "fsdp"
D = 1024
HALF = D // 2
QUERY_HEADS = 16
KEY_VALUE_HEADS = 8
HEAD_SIZE = 128
FF = 3072
PART = FF // 2
GROUP = QUERY_HEADS // KEY_VALUE_HEADS
QW = QUERY_HEADS * HEAD_SIZE
KW = KEY_VALUE_HEADS * HEAD_SIZE
LONGEST = 512
BLK = 256
COLS = 512
STEP = 256
MLP_COLS = 3 * PART
PAIR = GROUP * HEAD_SIZE
EPS = 1e-06
THETA = 1000000.0
ROOT = math.sqrt(HEAD_SIZE)
SCALE2 = math.log2(math.e) / ROOT
VMEM = 56 * 1024 * 1024
F32 = jnp.float32
B16 = jnp.bfloat16


def axes_of(n):
    out, stride = [(1, 2)], 2
    for radix in (2, 2, 4, 4, 4, 4):
        if stride * radix <= n:
            out.append((stride, radix))
            stride *= radix
    while stride < n:
        out.append((stride, 2))
        stride *= 2
    return out


def move(value, n, axis, k):
    s, r = axis
    pairs = [(i, i + ((i // s % r + k) % r - i // s % r) * s) for i in range(n)]
    return lax.ppermute(value, AX, pairs)


def gather_chain(value, n, ends_first=True):
    ax = axes_of(n)[1:]
    m = len(ax)
    rows, cols = value.shape
    h = rows // 2
    cur = value.reshape((1,) * m + (rows, cols))
    if ends_first:
        for a in range(2, m):
            s = yield [move(cur, n, ax[a], -k) for k in range(1, ax[a][1])]
            cur = jnp.concatenate([cur] + s, axis=a)
    parts = [cur[..., :h, :], cur[..., h:, :]]
    for pair in ((0, 1), (1, 0)):
        s = yield [move(u, n, ax[a], -1) for u, a in zip(parts, pair)]
        parts = [jnp.concatenate([u, w], axis=a) for u, w, a in zip(parts, s, pair)]
    cur = jnp.stack(parts)
    if not ends_first:
        for a in range(2, m):
            got = [cur]
            for _ in range(ax[a][1] - 1):
                got += yield [move(got[-1], n, ax[a], -1)]
            cur = jnp.concatenate(got, axis=a + 1)
    cur = cur.reshape(rows * n // 2, cols)
    s = yield [move(cur, n, (1, 2), 1)]
    return [cur] + s


def scatter_chain(blocks, n):
    ax = axes_of(n)[1:]
    cols = blocks[0].shape[1]
    h = D // n // 2
    keep, give = blocks
    (s,) = yield [move(give, n, (1, 2), 1)]
    acc = (keep.astype(F32) + s.astype(F32)).astype(B16)
    acc = acc.reshape((2,) + tuple(r for _, r in ax) + (h, cols))
    parts = [acc[0], acc[1]]

    def part(u, j, a):
        return lax.index_in_dim(u, j, a, keepdims=True)

    for pair in ((0, 1), (1, 0)):
        s = yield [move(part(u, 1, a), n, ax[a], 1) for u, a in zip(parts, pair)]
        parts = [
            (part(u, 0, a).astype(F32) + w.astype(F32)).astype(B16) for u, w, a in zip(parts, s, pair)
        ]
    acc = jnp.stack(parts)
    for a in range(len(ax) - 1, 1, -1):
        r = ax[a][1]
        s = yield [move(part(acc, k, a + 1), n, ax[a], k) for k in range(1, r)]
        terms = [part(acc, 0, a + 1)] + s
        acc = sum(u.astype(F32) for u in terms).astype(B16)
    return [u.reshape(2 * h, cols) for u in terms]


class Chain:
    def __init__(self, steps, stages=0):
        self.steps, self.sent, self.value, self.stages = steps, None, None, stages

    def start(self):
        if self.value is not None:
            return
        try:
            self.sent = self.steps.send(self.sent)
            self.stages -= 1
        except StopIteration as end:
            self.sent, self.value = None, end.value


def window(start, wait, *values):
    for c in start:
        c.start()
    live = [c for c in wait if c.sent is not None]
    if not live:
        return values
    sent, values = lax.optimization_barrier(([c.sent for c in live], values))
    for c, u in zip(live, sent):
        c.sent = u
    return values


def finish(*chains):
    while any(c.value is None for c in chains):
        left = [c for c in chains if c.value is None]
        window(left, left)


def absolute_rows(n):
    ax = axes_of(n)
    me = lax.axis_index(AX)
    share = D // n
    h = share // 2
    place = lax.broadcasted_iota(jnp.int32, (D,), 0)
    inner = place % h
    rem = place // h
    owner = jnp.zeros_like(place)
    for s, r in ax[:0:-1]:
        owner = owner + ((me // s + rem % r) % r) * s
        rem = rem // r
    owner = owner + (me + rem // 2) % 2
    return owner * share + (rem % 2) * h + inner


def sum_chain(value, n):
    step = 1
    while step < n:
        masks = (1, 2, 3) if 4 * step <= n else (1,)
        got = yield [lax.ppermute(value, AX, [(i, i ^ (m * step)) for i in range(n)]) for m in masks]
        value = value + got[0]
        if len(got) > 1:
            value = value + (got[1] + got[2])
        step *= len(masks) + 1
    return value


def call(kernel, grid, ins, outs, shapes, scratch=(), flops=0, moved=0, name=None):
    return pl.pallas_call(
        kernel,
        grid=grid,
        in_specs=ins,
        out_specs=outs,
        out_shape=shapes,
        scratch_shapes=list(scratch),
        compiler_params=pltpu.CompilerParams(vmem_limit_bytes=VMEM),
        cost_estimate=pl.CostEstimate(flops=flops, bytes_accessed=moved, transcendentals=0),
        name=name,
    )


def whole(shape):
    return pl.BlockSpec(shape, lambda *_: (0,) * len(shape))


def rows_of(cols, blk=BLK):
    return pl.BlockSpec((blk, cols), lambda i: (i, 0))


def sds(shape, dtype):
    return jax.ShapeDtypeStruct(shape, dtype)


def nn(a, b):
    return lax.dot_general(a, b, (((1,), (0,)), ((), ())), preferred_element_type=F32)


def nt(a, b):
    return lax.dot_general(a, b, (((1,), (1,)), ((), ())), preferred_element_type=F32)


def inv_rms(x):
    return lax.rsqrt(jnp.mean(x * x, axis=-1, keepdims=True) + EPS)


def chained(kernel, grid, ins, args, outs, shapes, before, scratch=(), flops=0, moved=0, name=None):
    if before is None or isinstance(before, dict):
        before = before or {}
    else:
        before = dict(enumerate(before))
    extra = list(before.values())
    n_in, n_extra = len(ins), len(extra)

    def body(*refs):
        kernel(*refs[:n_in], *refs[n_in + n_extra :])

    return pl.pallas_call(
        body,
        grid=grid,
        in_specs=list(ins) + [pl.BlockSpec(memory_space=pl.ANY)] * n_extra,
        out_specs=outs,
        out_shape=shapes,
        scratch_shapes=list(scratch),
        input_output_aliases={n_in + i: place for i, place in enumerate(before)},
        compiler_params=pltpu.CompilerParams(vmem_limit_bytes=VMEM),
        cost_estimate=pl.CostEstimate(flops=flops, bytes_accessed=moved, transcendentals=0),
        name=name,
    )(*args, *extra)


def halves_of(cols, where):
    return [pl.BlockSpec((HALF, cols), lambda j: (0, where(j)))] * 2


def joined(refs):
    return jnp.concatenate([r[...] for r in refs], axis=0)


def chunks(t):
    return [slice(i * BLK, (i + 1) * BLK) for i in range(t // BLK)]


def prep_kernel(tok, cot, perm, trel, crel, crel_t):
    trel[...] = nn(tok[...], perm[...]).astype(B16)
    c = nn(cot[...], perm[...]).astype(B16)
    crel[...] = c
    crel_t[...] = c.T


def prep(tokens, cotangent, perm):
    t = tokens.shape[0]
    return call(
        prep_kernel,
        (t // BLK,),
        [rows_of(D), rows_of(D), whole((D, D))],
        [rows_of(D), rows_of(D), pl.BlockSpec((D, BLK), lambda i: (0, i))],
        [sds((t, D), B16), sds((t, D), B16), sds((D, t), B16)],
        flops=4 * t * D * D,
        moved=12 * t * D,
        name="prep",
    )(tokens, cotangent, perm)


def head_rows(n1, w, cos, sin, gain, out, raw):
    for at in chunks(n1.shape[0]):
        x = nn(n1[at, :], w)
        raw[at, :] = x.astype(B16)
        for h in range(COLS // HEAD_SIZE):
            lanes = slice(h * HEAD_SIZE, (h + 1) * HEAD_SIZE)
            y = x[:, lanes]
            y = y * inv_rms(y) * gain[...]
            y = y * cos[at, :] + pltpu.roll(y, HEAD_SIZE // 2, 1) * sin[at, :]
            out[at, lanes] = y.astype(B16)


def queries_kernel(trel, gain, w0, w1, cos, sin, qg, q, rawq, n1, n1_t):
    @pl.when(pl.program_id(0) == 0)
    def _():
        for at in chunks(trel.shape[0]):
            x = trel[at, :].astype(F32)
            x = (x * inv_rms(x) * gain[...]).astype(B16)
            n1[at, :] = x
            n1_t[:, at] = x.T

    head_rows(n1, joined((w0, w1)), cos, sin, qg, q, rawq)


def project_queries(trel, gain, w, cos, sin, qg):
    t = trel.shape[0]
    table, one = whole((t, HEAD_SIZE)), whole((1, HEAD_SIZE))
    out = pl.BlockSpec((t, COLS), lambda j: (0, j))
    return call(
        queries_kernel,
        (QW // COLS,),
        [whole((t, D)), whole((1, D))] + halves_of(COLS, lambda j: j) + [table, table, one],
        [out, out, whole((t, D)), whole((D, t))],
        [sds((t, QW), B16)] * 2 + [sds((t, D), B16), sds((D, t), B16)],
        flops=2 * t * D * QW,
        moved=2 * (D * QW + t * (2 * QW + 3 * D)),
        name="project_queries",
    )(trel, gain, *w, cos, sin, qg)


def keys_kernel(n1, w0, w1, cos, sin, kg, k, rawk, v):
    w = joined((w0, w1))

    @pl.when(pl.program_id(0) < KW // COLS)
    def _():
        head_rows(n1, w, cos, sin, kg, k, rawk)

    @pl.when(pl.program_id(0) >= KW // COLS)
    def _():
        for at in chunks(n1.shape[0]):
            v[at, :] = nn(n1[at, :], w).astype(B16)


def project_keys(n1, w, cos, sin, kg):
    t = n1.shape[0]
    nk = KW // COLS
    table, one = whole((t, HEAD_SIZE)), whole((1, HEAD_SIZE))
    early = pl.BlockSpec((t, COLS), lambda j: (0, jnp.minimum(j, nk - 1)))
    late = pl.BlockSpec((t, COLS), lambda j: (0, jnp.maximum(j - nk, 0)))
    return call(
        keys_kernel,
        (2 * nk,),
        [whole((t, D))] + halves_of(COLS, lambda j: QW // COLS + j) + [table, table, one],
        [early, early, late],
        [sds((t, KW), B16)] * 3,
        flops=4 * t * D * KW,
        moved=2 * (2 * D * KW + t * (3 * KW + D)),
        name="project_keys",
    )(n1, *w, cos, sin, kg)


def build_bias(first, bias):
    t = bias.shape[0]
    for i, at in enumerate(chunks(t)):
        key = lax.broadcasted_iota(jnp.int32, (t, BLK), 0)
        query = lax.broadcasted_iota(jnp.int32, (t, BLK), 1) + i * BLK
        allowed = (key >= first[:, at]) & (key <= query)
        bias[:, at] = jnp.where(allowed, 0.0, -1e30)


def window_of(i):
    return slice(max(0, i - LONGEST // BLK) * BLK, (i + 1) * BLK)


def stacked(ref, at):
    return jnp.concatenate([ref[at, :HEAD_SIZE], ref[at, HEAD_SIZE:]], axis=0)


def attend_kernel(q, k, v, first, out, lse, bias):
    @pl.when(pl.program_id(0) == 0)
    def _():
        build_bias(first, bias)

    vt = v[...].T
    for i, at in enumerate(chunks(q.shape[0])):
        keys = window_of(i)
        s = nt(k[keys, :], stacked(q, at))
        b = bias[keys, at]
        e = jnp.exp2(s * SCALE2 + jnp.concatenate([b, b], axis=1))
        total = jnp.sum(e, axis=0, keepdims=True)
        o = (nn(vt[:, keys], e.astype(B16)) * (1.0 / total)).T.astype(B16)
        level = jnp.log2(total)
        for r in range(GROUP):
            mine = slice(r * BLK, (r + 1) * BLK)
            out[at, r * HEAD_SIZE : (r + 1) * HEAD_SIZE] = o[mine, :]
            lse[0, r : r + 1, at] = level[:, mine]


def attend(q, k, v, first):
    t = k.shape[0]
    groups = k.shape[1] // HEAD_SIZE
    head = pl.BlockSpec((t, HEAD_SIZE), lambda g: (0, g))
    both = pl.BlockSpec((t, PAIR), lambda g: (0, g))
    return call(
        attend_kernel,
        (groups,),
        [both, head, head, whole((1, t))],
        [both, pl.BlockSpec((1, GROUP, t), lambda g: (g, 0, 0))],
        [sds((t, groups * PAIR), B16), sds((groups, GROUP, t), F32)],
        [pltpu.VMEM((t, t), F32)],
        flops=8 * groups * t * t * PAIR,
        moved=12 * t * groups * HEAD_SIZE,
        name="attend",
    )(q, k, v, first)


def after_kernel(o, w0, w1, trel, gain, x1, n2, n2_t):
    j = pl.program_id(0)

    @pl.when(j == 0)
    def _():
        x1[...] = trel[...].astype(F32)

    w = joined((w0, w1))
    for at in chunks(o.shape[0]):
        x1[at, :] += nt(o[at, :], w)

    @pl.when(j == pl.num_programs(0) - 1)
    def _():
        for at in chunks(o.shape[0]):
            x = x1[at, :]
            y = (x * inv_rms(x) * gain[...]).astype(B16)
            n2[at, :] = y
            n2_t[:, at] = y.T


def after_attention(o, w, trel, gain):
    t = o.shape[0]
    return call(
        after_kernel,
        (QW // COLS,),
        [pl.BlockSpec((t, COLS), lambda j: (0, j))]
        + halves_of(COLS, lambda j: MLP_COLS // COLS + j)
        + [whole((t, D)), whole((1, D))],
        [whole((t, D)), whole((t, D)), whole((D, t))],
        [sds((t, D), F32), sds((t, D), B16), sds((D, t), B16)],
        flops=2 * t * D * QW,
        moved=2 * (t * QW + D * QW + 5 * t * D),
        name="after_attention",
    )(o, *w, trel, gain)


def mlp_kernel(n2, n2_t, c, c_t, w0, w1, hidden, dact, g0, g1):
    w = joined((w0, w1))
    for at in chunks(n2.shape[0]):
        x = nn(n2[at, :], w[:, STEP:])
        gate, up = x[:, :STEP], x[:, STEP:]
        dh = nn(c[at, :], w[:, :STEP])
        sig = jax.nn.sigmoid(gate)
        silu = gate * sig
        hidden[at, :] = (silu * up).astype(B16)
        dact[at, :STEP] = (dh * up * sig * (1.0 + gate * (1.0 - sig))).astype(B16)
        dact[at, STEP:] = (dh * silu).astype(B16)
    for p, out in enumerate((g0, g1)):
        mine = slice(p * HALF, (p + 1) * HALF)
        out[:, :STEP] = nn(c_t[mine, :], hidden[...]).astype(B16)
        out[:, STEP:] = nn(n2_t[mine, :], dact[...]).astype(B16)


def mlp(n2, n2_t, c, c_t, w, base, steps, cols, before):
    t = n2.shape[0]

    def at(width):
        return pl.BlockSpec((t, width), lambda j: (0, base + j))

    return chained(
        mlp_kernel,
        (steps,),
        [whole((t, D)), whole((D, t))] * 2 + halves_of(3 * STEP, lambda j: base + j),
        [n2, n2_t, c, c_t, *w],
        [at(STEP), at(2 * STEP)] + halves_of(3 * STEP, lambda j: base + j),
        [sds((t, PART), B16), sds((t, 2 * PART), B16)] + [sds((HALF, cols), B16)] * 2,
        before,
        flops=12 * t * D * STEP * steps,
        moved=8 * t * D + steps * STEP * (12 * D + 6 * t),
        name="mlp",
    )


def mlp_back0_kernel(x1, hidden, dact, w0, w1, dn2, res):
    @pl.when(pl.program_id(0) == 0)
    def _():
        dn2[...] = jnp.zeros_like(dn2)
        res[...] = x1[...]

    w = joined((w0, w1))
    for at in chunks(x1.shape[0]):
        dn2[at, :] += nt(dact[at, :], w[:, STEP:])
        res[at, :] += nt(hidden[at, :], w[:, :STEP])


def mlp_back0(x1, hidden, dact, w):
    t = x1.shape[0]

    def at(width):
        return pl.BlockSpec((t, width), lambda j: (0, j))

    return call(
        mlp_back0_kernel,
        (PART // STEP,),
        [whole((t, D)), at(STEP), at(2 * STEP)] + halves_of(3 * STEP, lambda j: j),
        [whole((t, D)), whole((t, D))],
        [sds((t, D), F32)] * 2,
        flops=6 * t * D * PART,
        moved=12 * t * D + 6 * PART * (t + D),
        name="mlp_back0",
    )(x1, hidden, dact, *w)


def mlp_back1_kernel(x1, crel, gain, dn2, dact, w0, w1, dx1, datt, datt_t):
    j = pl.program_id(0)
    w = joined((w0, w1))[:, STEP:]

    @pl.when(j == 0)
    def _():
        dx1[...] = dn2[...]

    for at in chunks(x1.shape[0]):
        dx1[at, :] += nt(dact[at, :], w)

    @pl.when(j == pl.num_programs(0) - 1)
    def _():
        for at in chunks(x1.shape[0]):
            x = x1[at, :]
            s = inv_rms(x)
            r = x * s
            grad = dx1[at, :] * gain[...]
            inner = jnp.mean(grad * r, axis=-1, keepdims=True)
            d = crel[at, :].astype(F32) + s * (grad - r * inner)
            dx1[at, :] = d
            low = d.astype(B16)
            datt[at, :] = low
            datt_t[:, at] = low.T


def mlp_back1(x1, crel, gain, dn2, dact, w):
    t = x1.shape[0]
    return call(
        mlp_back1_kernel,
        (PART // STEP,),
        [whole((t, D)), whole((t, D)), whole((1, D)), whole((t, D)),
         pl.BlockSpec((t, 2 * STEP), lambda j: (0, j))] + halves_of(3 * STEP, lambda j: j),
        [whole((t, D)), whole((t, D)), whole((D, t))],
        [sds((t, D), F32), sds((t, D), B16), sds((D, t), B16)],
        flops=4 * t * D * PART,
        moved=18 * t * D + 4 * PART * (t + D),
        name="mlp_back1",
    )(x1, crel, gain, dn2, dact, *w)


def out_grad_kernel(datt_t, o, g0, g1):
    for p, out in enumerate((g0, g1)):
        out[...] = nn(datt_t[p * HALF : (p + 1) * HALF, :], o[...]).astype(B16)


def out_grad(datt_t, o):
    t = o.shape[0]
    return chained(
        out_grad_kernel,
        (QW // COLS,),
        [whole((D, t)), pl.BlockSpec((t, COLS), lambda j: (0, j))],
        [datt_t, o],
        halves_of(COLS, lambda j: j),
        [sds((HALF, 2 * QW), B16)] * 2,
        None,
        flops=2 * t * D * QW,
        moved=2 * (t * D + t * QW + D * QW),
        name="out_grad",
    )


def result_kernel(res, perm, hidden, w0, w1, out, acc):
    j = pl.program_id(0)

    @pl.when(j == 0)
    def _():
        acc[...] = res[...]

    w = joined((w0, w1))
    for at in chunks(res.shape[0]):
        acc[at, :] += nt(hidden[at, :], w)

    @pl.when(j == pl.num_programs(0) - 1)
    def _():
        for at in chunks(res.shape[0]):
            out[at, :] = nt(acc[at, :].astype(B16), perm[...]).astype(B16)


def make_result(res, perm, hidden, w):
    t = res.shape[0]
    return call(
        result_kernel,
        (PART // STEP,),
        [whole((t, D)), whole((D, D)), pl.BlockSpec((t, STEP), lambda j: (0, j))]
        + halves_of(STEP, lambda j: 3 * j),
        whole((t, D)),
        sds((t, D), B16),
        [pltpu.VMEM((t, D), F32)],
        flops=2 * t * D * (PART + D),
        moved=2 * (t * PART + D * PART + 3 * t * D + D * D),
        name="result",
    )(res, perm, hidden, *w)


def head_back(dy, raw, cos, sin, gain):
    dn = dy * cos - pltpu.roll(dy, HEAD_SIZE // 2, 1) * sin
    x = raw.astype(F32)
    s = inv_rms(x)
    r = x * s
    grad = dn * gain
    inner = jnp.mean(grad * r, axis=-1, keepdims=True)
    return (s * (grad - r * inner)).astype(B16), jnp.sum(dn * r, axis=0, keepdims=True)


def attend_back_kernel(
    datt, n1_t, w0, w1, q, k, v, rawq, rawk, lse, first, cos, sin, qgain, kgain,
    gains, g0, g1, dq, dk, dv, bias, do, dk_sum, dv_sum, low,
):
    @pl.when(pl.program_id(0) == 0)
    def _():
        build_bias(first, bias)
        gains[...] = jnp.zeros_like(gains)

    t = q.shape[0]
    w = joined((w0, w1))
    for at in chunks(t):
        do[at, :] = nn(datt[at, :], w).astype(B16)
    kt = k[...].T
    dk_sum[...] = jnp.zeros_like(dk_sum)
    dv_sum[...] = jnp.zeros_like(dv_sum)
    for i, at in enumerate(chunks(t)):
        keys = window_of(i)
        q2, do2 = stacked(q, at), stacked(do, at)
        b = bias[keys, at]
        level = jnp.concatenate([lse[0, r : r + 1, at] for r in range(GROUP)], axis=1)
        s = nt(k[keys, :], q2)
        p = jnp.exp2(s * SCALE2 + jnp.concatenate([b, b], axis=1) - level)
        dp = nt(v[keys, :], do2)
        delta = jnp.sum(dp * p, axis=0, keepdims=True)
        ds = (p * (dp - delta)).astype(B16)
        dv_sum[keys, :] += nn(p.astype(B16), do2)
        dk_sum[keys, :] += nn(ds, q2)
        dq2 = nn(kt[:, keys], ds).T * (1.0 / ROOT)
        for r in range(GROUP):
            lanes = slice(r * HEAD_SIZE, (r + 1) * HEAD_SIZE)
            grad, part = head_back(
                dq2[r * BLK : (r + 1) * BLK, :], rawq[at, lanes], cos[at, :], sin[at, :], qgain[...]
            )
            low[at, lanes] = grad
            gains[0:1, :] += part
    for at in chunks(t):
        grad, part = head_back(
            dk_sum[at, :] * (1.0 / ROOT), rawk[at, :], cos[at, :], sin[at, :], kgain[...]
        )
        low[at, PAIR : PAIR + HEAD_SIZE] = grad
        gains[1:2, :] += part
    low[:, PAIR + HEAD_SIZE :] = dv_sum[...].astype(B16)
    dq[...] = low[:, :PAIR]
    dk[...] = low[:, PAIR : PAIR + HEAD_SIZE]
    dv[...] = low[:, PAIR + HEAD_SIZE :]
    for p, out in enumerate((g0, g1)):
        out[...] = nn(n1_t[p * HALF : (p + 1) * HALF, :], low[...]).astype(B16)


def attend_back(datt, n1_t, w, q, k, v, rawq, rawk, lse, first, tables, base, count, before, grads):
    t = k.shape[0]
    groups = k.shape[1] // HEAD_SIZE
    per = groups // 2
    ahead = QW // (2 * PAIR) if base < per else 0
    head = pl.BlockSpec((t, HEAD_SIZE), lambda g: (0, base + g))
    both = pl.BlockSpec((t, PAIR), lambda g: (0, base + g))
    table, one = whole((t, HEAD_SIZE)), whole((1, HEAD_SIZE))
    shapes = [sds((8, HEAD_SIZE), F32)] + [sds((HALF, (ahead + per) * 2 * PAIR), B16)] * 2
    shapes += [sds((t, QW), B16), sds((t, KW), B16), sds((t, KW), B16)]
    earlier = {1 + i: u for i, u in enumerate(grads or ())}
    earlier.update({3 + i: u for i, u in enumerate(before or ())})
    return chained(
        attend_back_kernel,
        (count,),
        [whole((t, D)), whole((D, t))] + halves_of(PAIR, lambda g: MLP_COLS // PAIR + base + g)
        + [both, head, head, both, head, pl.BlockSpec((1, GROUP, t), lambda g: (base + g, 0, 0)),
           whole((1, t)), table, table, one, one],
        [datt, n1_t, *w, q, k, v, rawq, rawk, lse, first, *tables],
        [whole((8, HEAD_SIZE))] + halves_of(2 * PAIR, lambda g: ahead + (base + g) % per) + [both, head, head],
        shapes,
        earlier,
        [pltpu.VMEM((t, t), F32), pltpu.VMEM((t, PAIR), B16), pltpu.VMEM((t, HEAD_SIZE), F32),
         pltpu.VMEM((t, HEAD_SIZE), F32), pltpu.VMEM((t, 2 * PAIR), B16)],
        flops=count * (6 * t * D * PAIR + 10 * t * t * PAIR),
        moved=4 * t * D + count * (12 * t * HEAD_SIZE * 2 + 6 * D * PAIR),
        name="attend_back",
    )


def input_back_kernel(trel, dx1, gain, perm, dq, dk, dv, w0, w1, out):
    grad = jnp.concatenate(
        [
            nt(dq[...], w[:, :QW]) + nt(dk[...], w[:, QW : QW + KW]) + nt(dv[...], w[:, QW + KW :])
            for w in (w0, w1)
        ],
        axis=1,
    )
    x = trel[...].astype(F32)
    s = inv_rms(x)
    r = x * s
    grad = grad * gain[...]
    inner = jnp.mean(grad * r, axis=-1, keepdims=True)
    d = (dx1[...] + s * (grad - r * inner)).astype(B16)
    out[...] = nt(d, perm[...]).astype(B16)


def input_back(trel, dx1, gain, perm, dq, dk, dv, w):
    t = trel.shape[0]
    return call(
        input_back_kernel,
        (t // BLK,),
        [rows_of(D), rows_of(D), whole((1, D)), whole((D, D)), rows_of(QW), rows_of(KW), rows_of(KW)]
        + halves_of(QW + 2 * KW, lambda i: 0),
        rows_of(D),
        sds((t, D), B16),
        flops=2 * t * D * (QW + 2 * KW + D),
        moved=2 * (t * (QW + 2 * KW) + D * (QW + 2 * KW) + 4 * t * D + D * D),
        name="input_back",
    )(trel, dx1, gain, perm, dq, dk, dv, *w)


def added(refs, cols):
    return functools.reduce(lambda u, w: u + w, [r[:, cols].astype(F32) for r in refs])


def mlp_total_kernel(count, gain, wg, wu, *refs):
    sums, (down, gate, up, grad_gain) = (refs[:count], refs[count : 2 * count]), refs[2 * count :]
    total = jnp.zeros(grad_gain.shape, F32)
    for i, terms in enumerate(sums):
        for j in range(PART // STEP):
            x = added(terms, slice(3 * j * STEP, 3 * (j + 1) * STEP))
            at = slice(i * PART + j * STEP, i * PART + (j + 1) * STEP)
            down[:, at] = x[:, :STEP]
            gate[:, at] = x[:, STEP : 2 * STEP]
            up[:, at] = x[:, 2 * STEP :]
            both = wg[:, at].astype(F32) * x[:, STEP : 2 * STEP] + wu[:, at].astype(F32) * x[:, 2 * STEP :]
            total = total + jnp.sum(both, axis=1, keepdims=True)
    grad_gain[...] = total / gain[...].astype(F32)


def mlp_total(gain, wg, wu, first, second):
    share = wg.shape[0]
    ins = [gain.reshape(share, 1), wg, wu, *first, *second]
    shapes = [sds((share, FF), F32)] * 3 + [sds((share, 1), F32)]
    return call(
        functools.partial(mlp_total_kernel, len(first)),
        (1,),
        [whole(u.shape) for u in ins],
        [whole(u.shape) for u in shapes],
        shapes,
        moved=share * FF * 40,
        name="mlp_total",
    )(*ins)


def attn_total_kernel(count, gain, wq, wk, wv, *refs):
    early, late = refs[:count], refs[count : 2 * count]
    out, q, k, v, grad_gain = refs[2 * count :]
    out[...] = added(early, slice(0, QW))
    total = jnp.zeros(grad_gain.shape, F32)
    half = KEY_VALUE_HEADS // 2
    for g in range(KEY_VALUE_HEADS):
        terms, start = (early, QW + 2 * PAIR * g) if g < half else (late, 2 * PAIR * (g - half))
        x = added(terms, slice(start, start + 2 * PAIR))
        wide, head = slice(g * PAIR, (g + 1) * PAIR), slice(g * HEAD_SIZE, (g + 1) * HEAD_SIZE)
        q[:, wide] = x[:, :PAIR]
        k[:, head] = x[:, PAIR : PAIR + HEAD_SIZE]
        v[:, head] = x[:, PAIR + HEAD_SIZE :]
        w = jnp.concatenate([wq[:, wide], wk[:, head], wv[:, head]], axis=1)
        total = total + jnp.sum(w.astype(F32) * x, axis=1, keepdims=True)
    grad_gain[...] = total / gain[...].astype(F32)


def attn_total(gain, wq, wk, wv, early, late):
    share = wq.shape[0]
    ins = [gain.reshape(share, 1), wq, wk, wv, *early, *late]
    shapes = [sds((share, QW), F32)] * 2 + [sds((share, KW), F32)] * 2 + [sds((share, 1), F32)]
    return call(
        functools.partial(attn_total_kernel, len(early)),
        (1,),
        [whole(u.shape) for u in ins],
        [whole(u.shape) for u in shapes],
        shapes,
        moved=share * (QW + KW) * 40,
        name="attn_total",
    )(*ins)


def run_starts(segment_row):
    index = jnp.arange(segment_row.shape[0], dtype=jnp.int32)
    previous = jnp.concatenate([segment_row[:1] - 1, segment_row[:-1]])
    return index, lax.cummax(jnp.where(segment_row != previous, index, 0), axis=0)


def by_step(gate, up, down):
    rows = gate.shape[0]
    three = [w.reshape(rows, -1, 1, STEP) for w in (down, gate, up)]
    return jnp.concatenate(three, axis=2).reshape(rows, -1)


def per_device(
    n, tokens, segments, cotangent, w_query, w_key, w_value, w_out, w_gate, w_up, w_down,
    attn_gain, mlp_gain, q_gain, k_gain,
):
    share = D // n
    steps = PART // STEP
    count = len(axes_of(n))
    gain_cols = jnp.concatenate([attn_gain[:, None], mlp_gain[:, None]], axis=1)
    gain_cols = jnp.pad(gain_cols, ((0, 0), (0, HEAD_SIZE - 2)))
    down_t = w_down.T
    halves = [
        by_step(w_gate[:, cols], w_up[:, cols], down_t[:, cols])
        for cols in (slice(0, PART), slice(PART, FF))
    ]
    shards1 = jnp.concatenate([w_query, w_key, w_value, gain_cols], axis=1)
    shards2 = jnp.concatenate([halves[0], w_out.T], axis=1)
    chain1 = Chain(gather_chain(shards1, n), count)
    chain2 = Chain(gather_chain(shards2, n), count)
    chain3 = Chain(gather_chain(halves[1], n, ends_first=False), count)

    index, first = run_starts(segments[0])
    half = HEAD_SIZE // 2
    freq = THETA ** (-jnp.arange(half, dtype=F32) / half)
    turned = (index - first).astype(F32)[:, None] * freq[None, :]
    cos, sin = jnp.cos(turned), jnp.sin(turned)
    cos = jnp.concatenate([cos, cos], axis=1)
    sin = jnp.concatenate([-sin, sin], axis=1)
    first = first.reshape(1, -1)
    qg = q_gain.astype(F32).reshape(1, HEAD_SIZE)
    kg = k_gain.astype(F32).reshape(1, HEAD_SIZE)
    perm = (jnp.arange(D, dtype=jnp.int32)[:, None] == absolute_rows(n)[None, :]).astype(B16)

    window([chain1, chain3], [chain3])
    cos, sin, perm = window([chain3], [chain1, chain3], cos, sin, perm)
    while chain1.stages > 3:
        window([chain1], [chain1])
    tokens, cotangent = window([chain1, chain2], [chain1], tokens, cotangent)
    trel, crel, crel_t = prep(tokens, cotangent, perm)
    trel, crel, crel_t = window([chain1], [chain1, chain2], trel, crel, crel_t)
    while chain2.stages > 3:
        window([chain2], [chain2])
    window([chain1, chain2, chain3], [chain1])
    finish(chain1)
    w_in = chain1.value
    gains = jnp.concatenate([w[:, QW + 2 * KW :] for w in w_in], axis=0).astype(F32).T
    gain_a, gain_m = gains[0:1], gains[1:2]

    q, rawq, n1, n1_t = project_queries(trel, gain_a, w_in, cos, sin, qg)
    q, rawq, n1, n1_t = window([], [chain2], q, rawq, n1, n1_t)
    k, rawk, v = project_keys(n1, w_in, cos, sin, kg)
    k, rawk, v = window([chain2], [chain3], k, rawk, v)
    o, lse = attend(q, k, v, first)
    o, lse = window([chain3], [chain2], o, lse)
    window([chain2], [chain2, chain3])
    finish(chain2)
    x1, n2, n2_t = after_attention(o, chain2.value, trel, gain_m)

    def units(w, base, acts):
        return mlp(n2, n2_t, crel, crel_t, w, base, steps // 3, MLP_COLS, acts)

    acts = units(chain2.value, 0, None)
    acts = window([chain3], [chain3], *acts)
    while chain3.stages > 1:
        window([chain3], [chain3])
    acts = units(chain2.value, steps // 3, acts)
    acts = units(chain2.value, 2 * steps // 3, acts)
    acts = window([chain3], [chain3], *acts)
    finish(chain3)
    hidden0, dact0, *grads = acts
    sum1 = Chain(scatter_chain(grads, n))
    dn2, res = mlp_back0(x1, hidden0, dact0, chain2.value)
    dn2, res = window([sum1], [sum1], dn2, res)

    acts = units(chain3.value, 0, None)
    acts = units(chain3.value, steps // 3, acts)
    acts = window([sum1], [sum1], *acts)
    acts = units(chain3.value, 2 * steps // 3, acts)
    acts = window([sum1], [sum1], *acts)
    hidden1, dact1, *grads = acts
    sum2 = Chain(scatter_chain(grads, n))
    dx1, datt, datt_t = mlp_back1(x1, crel, gain_m, dn2, dact1, chain3.value)
    dx1, datt, datt_t = window([sum1, sum2], [sum2], dx1, datt, datt_t)

    tables = (cos, sin, qg, kg)
    per = KEY_VALUE_HEADS // 4

    def heads(i, before, grads):
        return attend_back(
            datt, n1_t, chain2.value, q, k, v, rawq, rawk, lse, first, tables,
            i * per, per, before, grads,
        )

    gain0, *rest = heads(0, None, out_grad(datt_t, o))
    gain0, *rest = window([sum2], [sum1, sum2], gain0, *rest)
    gain1, *rest = heads(1, rest[2:], rest[:2])
    gain1, *rest = window([sum2], [sum2], gain1, *rest)
    sum3 = Chain(scatter_chain(rest[:2], n))
    gain2, *rest = heads(2, rest[2:], None)
    gain2, *rest = window([sum2, sum3], [sum3], gain2, *rest)
    gain3, *rest = heads(3, rest[2:], rest[:2])
    gain3, res, *rest = window([sum3], [sum2, sum3], gain3, res, *rest)
    sum4 = Chain(scatter_chain(rest[:2], n))
    dq, dk, dv = rest[2:]
    total = Chain(sum_chain((gain0 + gain1) + (gain2 + gain3), n))
    result = make_result(res, perm, hidden1, chain3.value)
    result, dq, dk, dv = window([sum3, sum4, total], [sum3, sum4, total], result, dq, dk, dv)
    grad_tokens = input_back(trel, dx1, gain_a, perm, dq, dk, dv, w_in)
    (grad_tokens,) = window([sum4, sum3, total], [sum4, total], grad_tokens)
    window([sum4, total], [sum4, total])
    finish(sum1, sum2, sum3, sum4, total)

    grad_down, grad_gate, grad_up, grad_mlp_gain = mlp_total(
        mlp_gain, w_gate, w_up, sum1.value, sum2.value
    )
    grad_out, grad_query, grad_key, grad_value, grad_attn_gain = attn_total(
        attn_gain, w_query, w_key, w_value, sum3.value, sum4.value
    )
    return (
        result,
        grad_tokens,
        grad_query,
        grad_key,
        grad_value,
        grad_out.T,
        grad_gate,
        grad_up,
        grad_down.T,
        grad_attn_gain[:, 0],
        grad_mlp_gain[:, 0],
        total.value[0],
        total.value[1],
    )


def solution(mesh):
    n = mesh.shape[AX]
    rows, cols, one = P(AX, None), P(None, AX), P(AX)
    in_specs = (rows, rows, rows, rows, rows, rows, cols, rows, rows, cols, one, one, P(), P())
    out_specs = (rows, rows, rows, rows, rows, cols, rows, rows, cols, one, one, P(), P())
    return jax.shard_map(
        functools.partial(per_device, n), mesh=mesh, in_specs=in_specs, out_specs=out_specs, check_vma=False
    )
```

```python
import functools
import math

import jax
import jax.numpy as jnp
from jax import lax
from jax.experimental import pallas as pl
from jax.experimental.pallas import tpu as pltpu
from jax.sharding import PartitionSpec as P

AX = "fsdp"
D = 1024
HALF = D // 2
QUERY_HEADS = 16
KEY_VALUE_HEADS = 8
HEAD_SIZE = 128
FF = 3072
PART = FF // 2
GROUP = QUERY_HEADS // KEY_VALUE_HEADS
QW = QUERY_HEADS * HEAD_SIZE
KW = KEY_VALUE_HEADS * HEAD_SIZE
LONGEST = 512
BLK = 256
COLS = 512
STEP = 256
MLP_COLS = 3 * PART
PAIR = GROUP * HEAD_SIZE
EPS = 1e-06
THETA = 1000000.0
ROOT = math.sqrt(HEAD_SIZE)
SCALE2 = math.log2(math.e) / ROOT
VMEM = 56 * 1024 * 1024
F32 = jnp.float32
B16 = jnp.bfloat16


def axes_of(n):
    out, stride = [(1, 2)], 2
    for radix in (2, 2, 4, 4, 4, 4):
        if stride * radix <= n:
            out.append((stride, radix))
            stride *= radix
    while stride < n:
        out.append((stride, 2))
        stride *= 2
    return out


def move(value, n, axis, k):
    s, r = axis
    pairs = [(i, i + ((i // s % r + k) % r - i // s % r) * s) for i in range(n)]
    return lax.ppermute(value, AX, pairs)


def spread(values, n, axis, sign, split):
    places = list(range(1, len(values)))
    stages = [[k for k in places if k % 2 == 0], [k for k in places if k % 2]]
    got = {}
    for stage in stages if split and stages[0] else [places]:
        got.update(zip(stage, (yield [move(values[k], n, axis, sign * k) for k in stage])))
    return [got[k] for k in places]


def gather_chain(value, n, ends_first=True, ring=True):
    ax = axes_of(n)[1:]
    m = len(ax)
    rows, cols = value.shape
    h = rows // 2
    cur = value.reshape((1,) * m + (rows, cols))
    if ends_first:
        for a in range(2, m):
            if ring:
                got = [cur]
                for _ in range(ax[a][1] - 1):
                    got += yield [move(got[-1], n, ax[a], -1)]
            else:
                got = [cur] + (yield from spread([None] + [cur] * (ax[a][1] - 1), n, ax[a], -1, True))
            cur = jnp.concatenate(got, axis=a)
    parts = [cur[..., :h, :], cur[..., h:, :]]
    for pair in ((0, 1), (1, 0)):
        s = yield [move(u, n, ax[a], -1) for u, a in zip(parts, pair)]
        parts = [jnp.concatenate([u, w], axis=a) for u, w, a in zip(parts, s, pair)]
    cur = jnp.stack(parts)
    if not ends_first:
        for a in range(2, m):
            got = [cur]
            for _ in range(ax[a][1] - 1):
                got += yield [move(got[-1], n, ax[a], -1)]
            cur = jnp.concatenate(got, axis=a + 1)
    cur = cur.reshape(rows * n // 2, cols)
    s = yield [move(cur, n, (1, 2), 1)]
    return [cur] + s


def scatter_chain(blocks, n, split=True):
    ax = axes_of(n)[1:]
    cols = blocks[0].shape[1]
    h = D // n // 2
    keep, give = blocks
    (s,) = yield [move(give, n, (1, 2), 1)]
    acc = (keep.astype(F32) + s.astype(F32)).astype(B16)
    acc = acc.reshape((2,) + tuple(r for _, r in ax) + (h, cols))
    parts = [acc[0], acc[1]]

    def part(u, j, a):
        return lax.index_in_dim(u, j, a, keepdims=True)

    for pair in ((0, 1), (1, 0)):
        s = yield [move(part(u, 1, a), n, ax[a], 1) for u, a in zip(parts, pair)]
        parts = [
            (part(u, 0, a).astype(F32) + w.astype(F32)).astype(B16) for u, w, a in zip(parts, s, pair)
        ]
    acc = jnp.stack(parts)
    for a in range(len(ax) - 1, 1, -1):
        r = ax[a][1]
        s = yield from spread([part(acc, k, a + 1) for k in range(r)], n, ax[a], 1, split)
        terms = [part(acc, 0, a + 1)] + s
        acc = sum(u.astype(F32) for u in terms).astype(B16)
    return [u.reshape(2 * h, cols) for u in terms]


class Chain:
    def __init__(self, steps, stages=0):
        self.steps, self.sent, self.value, self.stages = steps, None, None, stages

    def start(self):
        if self.value is not None:
            return
        try:
            self.sent = self.steps.send(self.sent)
            self.stages -= 1
        except StopIteration as end:
            self.sent, self.value = None, end.value


def window(start, wait, *values):
    for c in start:
        c.start()
    live = [c for c in wait if c.sent is not None]
    if not live:
        return values
    sent, values = lax.optimization_barrier(([c.sent for c in live], values))
    for c, u in zip(live, sent):
        c.sent = u
    return values


def finish(*chains):
    while any(c.value is None for c in chains):
        left = [c for c in chains if c.value is None]
        window(left, left)


def absolute_rows(n):
    ax = axes_of(n)
    me = lax.axis_index(AX)
    share = D // n
    h = share // 2
    place = lax.broadcasted_iota(jnp.int32, (D,), 0)
    inner = place % h
    rem = place // h
    owner = jnp.zeros_like(place)
    for s, r in ax[:0:-1]:
        owner = owner + ((me // s + rem % r) % r) * s
        rem = rem // r
    owner = owner + (me + rem // 2) % 2
    return owner * share + (rem % 2) * h + inner


def sum_chain(value, n):
    step = 1
    while step < n:
        masks = (1, 2, 3) if 4 * step <= n else (1,)
        got = yield [lax.ppermute(value, AX, [(i, i ^ (m * step)) for i in range(n)]) for m in masks]
        value = value + got[0]
        if len(got) > 1:
            value = value + (got[1] + got[2])
        step *= len(masks) + 1
    return value


def call(kernel, grid, ins, outs, shapes, scratch=(), flops=0, moved=0, name=None):
    return pl.pallas_call(
        kernel,
        grid=grid,
        in_specs=ins,
        out_specs=outs,
        out_shape=shapes,
        scratch_shapes=list(scratch),
        compiler_params=pltpu.CompilerParams(vmem_limit_bytes=VMEM),
        cost_estimate=pl.CostEstimate(flops=flops, bytes_accessed=moved, transcendentals=0),
        name=name,
    )


def whole(shape):
    return pl.BlockSpec(shape, lambda *_: (0,) * len(shape))


def rows_of(cols, blk=BLK):
    return pl.BlockSpec((blk, cols), lambda i: (i, 0))


def sds(shape, dtype):
    return jax.ShapeDtypeStruct(shape, dtype)


def nn(a, b):
    return lax.dot_general(a, b, (((1,), (0,)), ((), ())), preferred_element_type=F32)


def nt(a, b):
    return lax.dot_general(a, b, (((1,), (1,)), ((), ())), preferred_element_type=F32)


def inv_rms(x):
    return lax.rsqrt(jnp.mean(x * x, axis=-1, keepdims=True) + EPS)


def chained(kernel, grid, ins, args, outs, shapes, before, scratch=(), flops=0, moved=0, name=None):
    if before is None or isinstance(before, dict):
        before = before or {}
    else:
        before = dict(enumerate(before))
    extra = list(before.values())
    n_in, n_extra = len(ins), len(extra)

    def body(*refs):
        kernel(*refs[:n_in], *refs[n_in + n_extra :])

    return pl.pallas_call(
        body,
        grid=grid,
        in_specs=list(ins) + [pl.BlockSpec(memory_space=pl.ANY)] * n_extra,
        out_specs=outs,
        out_shape=shapes,
        scratch_shapes=list(scratch),
        input_output_aliases={n_in + i: place for i, place in enumerate(before)},
        compiler_params=pltpu.CompilerParams(vmem_limit_bytes=VMEM),
        cost_estimate=pl.CostEstimate(flops=flops, bytes_accessed=moved, transcendentals=0),
        name=name,
    )(*args, *extra)


def halves_of(cols, where):
    return [pl.BlockSpec((HALF, cols), lambda j: (0, where(j)))] * 2


def joined(refs):
    return jnp.concatenate([r[...] for r in refs], axis=0)


def chunks(t):
    return [slice(i * BLK, (i + 1) * BLK) for i in range(t // BLK)]


def prep_kernel(tok, cot, perm, trel, crel, crel_t):
    trel[...] = nn(tok[...], perm[...]).astype(B16)
    c = nn(cot[...], perm[...]).astype(B16)
    crel[...] = c
    crel_t[...] = c.T


def prep(tokens, cotangent, perm):
    t = tokens.shape[0]
    return call(
        prep_kernel,
        (t // BLK,),
        [rows_of(D), rows_of(D), whole((D, D))],
        [rows_of(D), rows_of(D), pl.BlockSpec((D, BLK), lambda i: (0, i))],
        [sds((t, D), B16), sds((t, D), B16), sds((D, t), B16)],
        flops=4 * t * D * D,
        moved=12 * t * D,
        name="prep",
    )(tokens, cotangent, perm)


def head_rows(n1, w, cos, sin, gain, out, raw):
    for at in chunks(n1.shape[0]):
        x = nn(n1[at, :], w)
        raw[at, :] = x.astype(B16)
        for h in range(COLS // HEAD_SIZE):
            lanes = slice(h * HEAD_SIZE, (h + 1) * HEAD_SIZE)
            y = x[:, lanes]
            y = y * inv_rms(y) * gain[...]
            y = y * cos[at, :] + pltpu.roll(y, HEAD_SIZE // 2, 1) * sin[at, :]
            out[at, lanes] = y.astype(B16)


def queries_kernel(trel, g0, g1, w0, w1, cos, sin, qg, q, rawq, n1, n1_t, gains):
    @pl.when(pl.program_id(0) == 0)
    def _():
        gains[...] = joined((g0, g1)).astype(F32).T[:8]
        gain = gains[0:1, :]
        for at in chunks(trel.shape[0]):
            x = trel[at, :].astype(F32)
            x = (x * inv_rms(x) * gain).astype(B16)
            n1[at, :] = x
            n1_t[:, at] = x.T

    head_rows(n1, joined((w0, w1)), cos, sin, qg, q, rawq)


def project_queries(trel, w, cos, sin, qg):
    t = trel.shape[0]
    table, one = whole((t, HEAD_SIZE)), whole((1, HEAD_SIZE))
    out = pl.BlockSpec((t, COLS), lambda j: (0, j))
    return call(
        queries_kernel,
        (QW // COLS,),
        [whole((t, D))] + halves_of(HEAD_SIZE, lambda j: 3 * QW // HEAD_SIZE)
        + halves_of(COLS, lambda j: j) + [table, table, one],
        [out, out, whole((t, D)), whole((D, t)), whole((8, D))],
        [sds((t, QW), B16)] * 2 + [sds((t, D), B16), sds((D, t), B16), sds((8, D), F32)],
        flops=2 * t * D * QW,
        moved=2 * (D * QW + t * (2 * QW + 3 * D)),
        name="project_queries",
    )(trel, *w, *w, cos, sin, qg)


def keys_kernel(n1, w0, w1, cos, sin, kg, k, rawk, v):
    w = joined((w0, w1))

    @pl.when(pl.program_id(0) < KW // COLS)
    def _():
        head_rows(n1, w, cos, sin, kg, k, rawk)

    @pl.when(pl.program_id(0) >= KW // COLS)
    def _():
        for at in chunks(n1.shape[0]):
            v[at, :] = nn(n1[at, :], w).astype(B16)


def project_keys(n1, w, cos, sin, kg):
    t = n1.shape[0]
    nk = KW // COLS
    table, one = whole((t, HEAD_SIZE)), whole((1, HEAD_SIZE))
    early = pl.BlockSpec((t, COLS), lambda j: (0, jnp.minimum(j, nk - 1)))
    late = pl.BlockSpec((t, COLS), lambda j: (0, jnp.maximum(j - nk, 0)))
    return call(
        keys_kernel,
        (2 * nk,),
        [whole((t, D))] + halves_of(COLS, lambda j: QW // COLS + j) + [table, table, one],
        [early, early, late],
        [sds((t, KW), B16)] * 3,
        flops=4 * t * D * KW,
        moved=2 * (2 * D * KW + t * (3 * KW + D)),
        name="project_keys",
    )(n1, *w, cos, sin, kg)


def build_bias(first, bias):
    t = bias.shape[0]
    for i, at in enumerate(chunks(t)):
        key = lax.broadcasted_iota(jnp.int32, (t, BLK), 0)
        query = lax.broadcasted_iota(jnp.int32, (t, BLK), 1) + i * BLK
        allowed = (key >= first[:, at]) & (key <= query)
        bias[:, at] = jnp.where(allowed, 0.0, -1e30)


def window_of(i):
    return slice(max(0, i - LONGEST // BLK) * BLK, (i + 1) * BLK)


def stacked(ref, at):
    return jnp.concatenate([ref[at, :HEAD_SIZE], ref[at, HEAD_SIZE:]], axis=0)


def attend_kernel(q, k, v, first, out, lse, bias):
    @pl.when(pl.program_id(0) == 0)
    def _():
        build_bias(first, bias)

    vt = v[...].T
    for i, at in enumerate(chunks(q.shape[0])):
        keys = window_of(i)
        s = nt(k[keys, :], stacked(q, at))
        b = bias[keys, at]
        e = jnp.exp2(s * SCALE2 + jnp.concatenate([b, b], axis=1))
        total = jnp.sum(e, axis=0, keepdims=True)
        o = (nn(vt[:, keys], e.astype(B16)) * (1.0 / total)).T.astype(B16)
        level = jnp.log2(total)
        for r in range(GROUP):
            mine = slice(r * BLK, (r + 1) * BLK)
            out[at, r * HEAD_SIZE : (r + 1) * HEAD_SIZE] = o[mine, :]
            lse[0, r : r + 1, at] = level[:, mine]


def attend(q, k, v, first):
    t = k.shape[0]
    groups = k.shape[1] // HEAD_SIZE
    head = pl.BlockSpec((t, HEAD_SIZE), lambda g: (0, g))
    both = pl.BlockSpec((t, PAIR), lambda g: (0, g))
    return call(
        attend_kernel,
        (groups,),
        [both, head, head, whole((1, t))],
        [both, pl.BlockSpec((1, GROUP, t), lambda g: (g, 0, 0))],
        [sds((t, groups * PAIR), B16), sds((groups, GROUP, t), F32)],
        [pltpu.VMEM((t, t), F32)],
        flops=8 * groups * t * t * PAIR,
        moved=12 * t * groups * HEAD_SIZE,
        name="attend",
    )(q, k, v, first)


def after_kernel(o, w0, w1, trel, gain, x1, n2, n2_t):
    j = pl.program_id(0)

    @pl.when(j == 0)
    def _():
        x1[...] = trel[...].astype(F32)

    w = joined((w0, w1))
    for at in chunks(o.shape[0]):
        x1[at, :] += nt(o[at, :], w)

    @pl.when(j == pl.num_programs(0) - 1)
    def _():
        for at in chunks(o.shape[0]):
            x = x1[at, :]
            y = (x * inv_rms(x) * gain[...]).astype(B16)
            n2[at, :] = y
            n2_t[:, at] = y.T


def after_attention(o, w, trel, gain):
    t = o.shape[0]
    return call(
        after_kernel,
        (QW // COLS,),
        [pl.BlockSpec((t, COLS), lambda j: (0, j))]
        + halves_of(COLS, lambda j: 2 * QW // COLS + j)
        + [whole((t, D)), whole((1, D))],
        [whole((t, D)), whole((t, D)), whole((D, t))],
        [sds((t, D), F32), sds((t, D), B16), sds((D, t), B16)],
        flops=2 * t * D * QW,
        moved=2 * (t * QW + D * QW + 5 * t * D),
        name="after_attention",
    )(o, *w, trel, gain)


def mlp_kernel(n2, n2_t, c, c_t, w0, w1, hidden, dact, g0, g1):
    w = joined((w0, w1))
    for at in chunks(n2.shape[0]):
        x = nn(n2[at, :], w[:, STEP:])
        gate, up = x[:, :STEP], x[:, STEP:]
        dh = nn(c[at, :], w[:, :STEP])
        sig = jax.nn.sigmoid(gate)
        silu = gate * sig
        hidden[at, :] = (silu * up).astype(B16)
        dact[at, :STEP] = (dh * up * sig * (1.0 + gate * (1.0 - sig))).astype(B16)
        dact[at, STEP:] = (dh * silu).astype(B16)
    for p, out in enumerate((g0, g1)):
        mine = slice(p * HALF, (p + 1) * HALF)
        out[:, :STEP] = nn(c_t[mine, :], hidden[...]).astype(B16)
        out[:, STEP:] = nn(n2_t[mine, :], dact[...]).astype(B16)


def mlp(n2, n2_t, c, c_t, w, base, steps, cols, before):
    t = n2.shape[0]

    def at(width):
        return pl.BlockSpec((t, width), lambda j: (0, base + j))

    return chained(
        mlp_kernel,
        (steps,),
        [whole((t, D)), whole((D, t))] * 2 + halves_of(3 * STEP, lambda j: base + j),
        [n2, n2_t, c, c_t, *w],
        [at(STEP), at(2 * STEP)] + halves_of(3 * STEP, lambda j: base + j),
        [sds((t, PART), B16), sds((t, 2 * PART), B16)] + [sds((HALF, cols), B16)] * 2,
        before,
        flops=12 * t * D * STEP * steps,
        moved=8 * t * D + steps * STEP * (12 * D + 6 * t),
        name="mlp",
    )


def mlp_back0_kernel(x1, hidden, dact, w0, w1, dn2, res):
    @pl.when(pl.program_id(0) == 0)
    def _():
        dn2[...] = jnp.zeros_like(dn2)
        res[...] = x1[...]

    w = joined((w0, w1))
    for at in chunks(x1.shape[0]):
        dn2[at, :] += nt(dact[at, :], w[:, STEP:])
        res[at, :] += nt(hidden[at, :], w[:, :STEP])


def mlp_back0(x1, hidden, dact, w):
    t = x1.shape[0]

    def at(width):
        return pl.BlockSpec((t, width), lambda j: (0, j))

    return call(
        mlp_back0_kernel,
        (PART // STEP,),
        [whole((t, D)), at(STEP), at(2 * STEP)] + halves_of(3 * STEP, lambda j: j),
        [whole((t, D)), whole((t, D))],
        [sds((t, D), F32)] * 2,
        flops=6 * t * D * PART,
        moved=12 * t * D + 6 * PART * (t + D),
        name="mlp_back0",
    )(x1, hidden, dact, *w)


def mlp_back1_kernel(x1, crel, gain, dn2, dact, w0, w1, dx1, datt, datt_t):
    j = pl.program_id(0)
    w = joined((w0, w1))[:, STEP:]

    @pl.when(j == 0)
    def _():
        dx1[...] = dn2[...]

    for at in chunks(x1.shape[0]):
        dx1[at, :] += nt(dact[at, :], w)

    @pl.when(j == pl.num_programs(0) - 1)
    def _():
        for at in chunks(x1.shape[0]):
            x = x1[at, :]
            s = inv_rms(x)
            r = x * s
            grad = dx1[at, :] * gain[...]
            inner = jnp.mean(grad * r, axis=-1, keepdims=True)
            d = crel[at, :].astype(F32) + s * (grad - r * inner)
            dx1[at, :] = d
            low = d.astype(B16)
            datt[at, :] = low
            datt_t[:, at] = low.T


def mlp_back1(x1, crel, gain, dn2, dact, w):
    t = x1.shape[0]
    return call(
        mlp_back1_kernel,
        (PART // STEP,),
        [whole((t, D)), whole((t, D)), whole((1, D)), whole((t, D)),
         pl.BlockSpec((t, 2 * STEP), lambda j: (0, j))] + halves_of(3 * STEP, lambda j: j),
        [whole((t, D)), whole((t, D)), whole((D, t))],
        [sds((t, D), F32), sds((t, D), B16), sds((D, t), B16)],
        flops=4 * t * D * PART,
        moved=18 * t * D + 4 * PART * (t + D),
        name="mlp_back1",
    )(x1, crel, gain, dn2, dact, *w)


def out_grad_kernel(datt_t, o, g0, g1):
    for p, out in enumerate((g0, g1)):
        out[...] = nn(datt_t[p * HALF : (p + 1) * HALF, :], o[...]).astype(B16)


def out_grad(datt_t, o):
    t = o.shape[0]
    return chained(
        out_grad_kernel,
        (QW // COLS,),
        [whole((D, t)), pl.BlockSpec((t, COLS), lambda j: (0, j))],
        [datt_t, o],
        halves_of(COLS, lambda j: j),
        [sds((HALF, 2 * QW), B16)] * 2,
        None,
        flops=2 * t * D * QW,
        moved=2 * (t * D + t * QW + D * QW),
        name="out_grad",
    )


def result_kernel(res, perm, hidden, w0, w1, out, acc):
    j = pl.program_id(0)

    @pl.when(j == 0)
    def _():
        acc[...] = res[...]

    w = joined((w0, w1))
    for at in chunks(res.shape[0]):
        acc[at, :] += nt(hidden[at, :], w)

    @pl.when(j == pl.num_programs(0) - 1)
    def _():
        for at in chunks(res.shape[0]):
            out[at, :] = nt(acc[at, :].astype(B16), perm[...]).astype(B16)


def make_result(res, perm, hidden, w):
    t = res.shape[0]
    return call(
        result_kernel,
        (PART // STEP,),
        [whole((t, D)), whole((D, D)), pl.BlockSpec((t, STEP), lambda j: (0, j))]
        + halves_of(STEP, lambda j: 3 * j),
        whole((t, D)),
        sds((t, D), B16),
        [pltpu.VMEM((t, D), F32)],
        flops=2 * t * D * (PART + D),
        moved=2 * (t * PART + D * PART + 3 * t * D + D * D),
        name="result",
    )(res, perm, hidden, *w)


def head_back(dy, raw, cos, sin, gain):
    dn = dy * cos - pltpu.roll(dy, HEAD_SIZE // 2, 1) * sin
    x = raw.astype(F32)
    s = inv_rms(x)
    r = x * s
    grad = dn * gain
    inner = jnp.mean(grad * r, axis=-1, keepdims=True)
    return (s * (grad - r * inner)).astype(B16), jnp.sum(dn * r, axis=0, keepdims=True)


def attend_back_kernel(
    datt, n1_t, w0, w1, q, k, v, rawq, rawk, lse, first, cos, sin, qgain, kgain,
    gains, g0, g1, dq, dk, dv, bias, do, dk_sum, dv_sum, low,
):
    @pl.when(pl.program_id(0) == 0)
    def _():
        build_bias(first, bias)
        gains[...] = jnp.zeros_like(gains)

    t = q.shape[0]
    w = joined((w0, w1))
    for at in chunks(t):
        do[at, :] = nn(datt[at, :], w).astype(B16)
    kt = k[...].T
    dk_sum[...] = jnp.zeros_like(dk_sum)
    dv_sum[...] = jnp.zeros_like(dv_sum)
    for i, at in enumerate(chunks(t)):
        keys = window_of(i)
        q2, do2 = stacked(q, at), stacked(do, at)
        b = bias[keys, at]
        level = jnp.concatenate([lse[0, r : r + 1, at] for r in range(GROUP)], axis=1)
        s = nt(k[keys, :], q2)
        p = jnp.exp2(s * SCALE2 + jnp.concatenate([b, b], axis=1) - level)
        dp = nt(v[keys, :], do2)
        delta = jnp.sum(dp * p, axis=0, keepdims=True)
        ds = (p * (dp - delta)).astype(B16)
        dv_sum[keys, :] += nn(p.astype(B16), do2)
        dk_sum[keys, :] += nn(ds, q2)
        dq2 = nn(kt[:, keys], ds).T * (1.0 / ROOT)
        for r in range(GROUP):
            lanes = slice(r * HEAD_SIZE, (r + 1) * HEAD_SIZE)
            grad, part = head_back(
                dq2[r * BLK : (r + 1) * BLK, :], rawq[at, lanes], cos[at, :], sin[at, :], qgain[...]
            )
            low[at, lanes] = grad
            gains[0:1, :] += part
    for at in chunks(t):
        grad, part = head_back(
            dk_sum[at, :] * (1.0 / ROOT), rawk[at, :], cos[at, :], sin[at, :], kgain[...]
        )
        low[at, PAIR : PAIR + HEAD_SIZE] = grad
        gains[1:2, :] += part
    low[:, PAIR + HEAD_SIZE :] = dv_sum[...].astype(B16)
    dq[...] = low[:, :PAIR]
    dk[...] = low[:, PAIR : PAIR + HEAD_SIZE]
    dv[...] = low[:, PAIR + HEAD_SIZE :]
    for p, out in enumerate((g0, g1)):
        out[...] = nn(n1_t[p * HALF : (p + 1) * HALF, :], low[...]).astype(B16)


def attend_back(datt, n1_t, w, q, k, v, rawq, rawk, lse, first, tables, base, count, before, grads):
    t = k.shape[0]
    groups = k.shape[1] // HEAD_SIZE
    per = groups // 2
    ahead = QW // (2 * PAIR) if base < per else 0
    head = pl.BlockSpec((t, HEAD_SIZE), lambda g: (0, base + g))
    both = pl.BlockSpec((t, PAIR), lambda g: (0, base + g))
    table, one = whole((t, HEAD_SIZE)), whole((1, HEAD_SIZE))
    shapes = [sds((8, HEAD_SIZE), F32)] + [sds((HALF, (ahead + per) * 2 * PAIR), B16)] * 2
    shapes += [sds((t, QW), B16), sds((t, KW), B16), sds((t, KW), B16)]
    earlier = {1 + i: u for i, u in enumerate(grads or ())}
    earlier.update({3 + i: u for i, u in enumerate(before or ())})
    return chained(
        attend_back_kernel,
        (count,),
        [whole((t, D)), whole((D, t))] + halves_of(PAIR, lambda g: 2 * QW // PAIR + base + g)
        + [both, head, head, both, head, pl.BlockSpec((1, GROUP, t), lambda g: (base + g, 0, 0)),
           whole((1, t)), table, table, one, one],
        [datt, n1_t, *w, q, k, v, rawq, rawk, lse, first, *tables],
        [whole((8, HEAD_SIZE))] + halves_of(2 * PAIR, lambda g: ahead + (base + g) % per) + [both, head, head],
        shapes,
        earlier,
        [pltpu.VMEM((t, t), F32), pltpu.VMEM((t, PAIR), B16), pltpu.VMEM((t, HEAD_SIZE), F32),
         pltpu.VMEM((t, HEAD_SIZE), F32), pltpu.VMEM((t, 2 * PAIR), B16)],
        flops=count * (6 * t * D * PAIR + 10 * t * t * PAIR),
        moved=4 * t * D + count * (12 * t * HEAD_SIZE * 2 + 6 * D * PAIR),
        name="attend_back",
    )


def input_back_kernel(trel, dx1, gain, perm, dq, dk, dv, w0, w1, out):
    grad = jnp.concatenate(
        [
            nt(dq[...], w[:, :QW]) + nt(dk[...], w[:, QW : QW + KW]) + nt(dv[...], w[:, QW + KW :])
            for w in (w0, w1)
        ],
        axis=1,
    )
    x = trel[...].astype(F32)
    s = inv_rms(x)
    r = x * s
    grad = grad * gain[...]
    inner = jnp.mean(grad * r, axis=-1, keepdims=True)
    d = (dx1[...] + s * (grad - r * inner)).astype(B16)
    out[...] = nt(d, perm[...]).astype(B16)


def input_back(trel, dx1, gain, perm, dq, dk, dv, w):
    t = trel.shape[0]
    return call(
        input_back_kernel,
        (t // BLK,),
        [rows_of(D), rows_of(D), whole((1, D)), whole((D, D)), rows_of(QW), rows_of(KW), rows_of(KW)]
        + halves_of(QW + 2 * KW, lambda i: 0),
        rows_of(D),
        sds((t, D), B16),
        flops=2 * t * D * (QW + 2 * KW + D),
        moved=2 * (t * (QW + 2 * KW) + D * (QW + 2 * KW) + 4 * t * D + D * D),
        name="input_back",
    )(trel, dx1, gain, perm, dq, dk, dv, *w)


def added(refs, cols):
    return functools.reduce(lambda u, w: u + w, [r[:, cols].astype(F32) for r in refs])


def mlp_total_kernel(count, gain, wg, wu, *refs):
    sums, (down, gate, up, grad_gain) = (refs[:count], refs[count : 2 * count]), refs[2 * count :]
    total = jnp.zeros(grad_gain.shape, F32)
    for i, terms in enumerate(sums):
        for j in range(PART // STEP):
            x = added(terms, slice(3 * j * STEP, 3 * (j + 1) * STEP))
            at = slice(i * PART + j * STEP, i * PART + (j + 1) * STEP)
            down[:, at] = x[:, :STEP]
            gate[:, at] = x[:, STEP : 2 * STEP]
            up[:, at] = x[:, 2 * STEP :]
            both = wg[:, at].astype(F32) * x[:, STEP : 2 * STEP] + wu[:, at].astype(F32) * x[:, 2 * STEP :]
            total = total + jnp.sum(both, axis=1, keepdims=True)
    grad_gain[...] = total / gain[...].astype(F32)


def mlp_total(gain, wg, wu, first, second):
    share = wg.shape[0]
    ins = [gain.reshape(share, 1), wg, wu, *first, *second]
    shapes = [sds((share, FF), F32)] * 3 + [sds((share, 1), F32)]
    return call(
        functools.partial(mlp_total_kernel, len(first)),
        (1,),
        [whole(u.shape) for u in ins],
        [whole(u.shape) for u in shapes],
        shapes,
        moved=share * FF * 40,
        name="mlp_total",
    )(*ins)


def attn_total_kernel(count, gain, wq, wk, wv, *refs):
    early, late = refs[:count], refs[count : 2 * count]
    out, q, k, v, grad_gain = refs[2 * count :]
    out[...] = added(early, slice(0, QW))
    total = jnp.zeros(grad_gain.shape, F32)
    half = KEY_VALUE_HEADS // 2
    for g in range(KEY_VALUE_HEADS):
        terms, start = (early, QW + 2 * PAIR * g) if g < half else (late, 2 * PAIR * (g - half))
        x = added(terms, slice(start, start + 2 * PAIR))
        wide, head = slice(g * PAIR, (g + 1) * PAIR), slice(g * HEAD_SIZE, (g + 1) * HEAD_SIZE)
        q[:, wide] = x[:, :PAIR]
        k[:, head] = x[:, PAIR : PAIR + HEAD_SIZE]
        v[:, head] = x[:, PAIR + HEAD_SIZE :]
        w = jnp.concatenate([wq[:, wide], wk[:, head], wv[:, head]], axis=1)
        total = total + jnp.sum(w.astype(F32) * x, axis=1, keepdims=True)
    grad_gain[...] = total / gain[...].astype(F32)


def attn_total(gain, wq, wk, wv, early, late):
    share = wq.shape[0]
    ins = [gain.reshape(share, 1), wq, wk, wv, *early, *late]
    shapes = [sds((share, QW), F32)] * 2 + [sds((share, KW), F32)] * 2 + [sds((share, 1), F32)]
    return call(
        functools.partial(attn_total_kernel, len(early)),
        (1,),
        [whole(u.shape) for u in ins],
        [whole(u.shape) for u in shapes],
        shapes,
        moved=share * (QW + KW) * 40,
        name="attn_total",
    )(*ins)


def run_starts(segment_row):
    index = jnp.arange(segment_row.shape[0], dtype=jnp.int32)
    previous = jnp.concatenate([segment_row[:1] - 1, segment_row[:-1]])
    return index, lax.cummax(jnp.where(segment_row != previous, index, 0), axis=0)


def by_step(gate, up, down):
    rows = gate.shape[0]
    three = [w.reshape(rows, -1, 1, STEP) for w in (down, gate, up)]
    return jnp.concatenate(three, axis=2).reshape(rows, -1)


def per_device(
    n, tokens, segments, cotangent, w_query, w_key, w_value, w_out, w_gate, w_up, w_down,
    attn_gain, mlp_gain, q_gain, k_gain,
):
    share = D // n
    steps = PART // STEP
    count = len(axes_of(n))
    gain_cols = jnp.concatenate([attn_gain[:, None], mlp_gain[:, None]], axis=1)
    gain_cols = jnp.pad(gain_cols, ((0, 0), (0, HEAD_SIZE - 2)))
    down_t = w_down.T
    halves = [
        by_step(w_gate[:, cols], w_up[:, cols], down_t[:, cols])
        for cols in (slice(0, PART), slice(PART, FF))
    ]
    shards1 = jnp.concatenate([w_query, w_key, w_value, w_out.T, gain_cols], axis=1)
    ends = [r for _, r in axes_of(n)[3:]]
    chain1 = Chain(gather_chain(shards1, n), 3 + sum(r - 1 for r in ends))
    chain2 = Chain(gather_chain(halves[0], n, ring=False), 3 + sum(1 + (r > 2) for r in ends))
    chain3 = Chain(gather_chain(halves[1], n, ends_first=False), 3 + sum(r - 1 for r in ends))

    index, first = run_starts(segments[0])
    half = HEAD_SIZE // 2
    freq = THETA ** (-jnp.arange(half, dtype=F32) / half)
    turned = (index - first).astype(F32)[:, None] * freq[None, :]
    cos, sin = jnp.cos(turned), jnp.sin(turned)
    cos = jnp.concatenate([cos, cos], axis=1)
    sin = jnp.concatenate([-sin, sin], axis=1)
    first = first.reshape(1, -1)
    qg = q_gain.astype(F32).reshape(1, HEAD_SIZE)
    kg = k_gain.astype(F32).reshape(1, HEAD_SIZE)
    perm = (jnp.arange(D, dtype=jnp.int32)[:, None] == absolute_rows(n)[None, :]).astype(B16)

    window([chain1, chain3], [chain1, chain3])
    cos, sin, perm = window([chain1, chain3], [chain1, chain3], cos, sin, perm)
    while chain1.stages > 3:
        window([chain1], [chain1])
    tokens, cotangent = window([chain1, chain2], [chain1, chain2], tokens, cotangent)
    while chain2.stages > 4:
        window([chain2], [chain2])
    every = [chain1, chain2, chain3]
    trel, crel, crel_t = prep(tokens, cotangent, perm)
    trel, crel, crel_t = window(every, every, trel, crel, crel_t)
    while chain3.stages > 3:
        window([chain3], [chain3])
    window([chain1, chain2], [chain1, chain2])
    finish(chain1)
    w_in = chain1.value

    q, rawq, n1, n1_t, gains = project_queries(trel, w_in, cos, sin, qg)
    gain_a, gain_m = gains[0:1], gains[1:2]
    k, rawk, v = project_keys(n1, w_in, cos, sin, kg)
    q, k, v = window([chain2, chain3], [chain2, chain3], q, k, v)
    o, lse = attend(q, k, v, first)
    o, lse = window([chain2], [chain2], o, lse)
    finish(chain2)
    x1, n2, n2_t = after_attention(o, w_in, trel, gain_m)

    def units(w, base, count, acts):
        return mlp(n2, n2_t, crel, crel_t, w, base, count, MLP_COLS, acts)

    acts = units(chain2.value, 0, steps, None)
    acts = window([chain3], [chain3], *acts)
    hidden0, dact0, *grads = acts
    sum1 = Chain(scatter_chain(grads, n))
    dn2, res = mlp_back0(x1, hidden0, dact0, chain2.value)
    dn2, res = window([chain3, sum1], [chain3, sum1], dn2, res)
    finish(chain3)

    acts = units(chain3.value, 0, steps, None)
    acts = window([sum1], [sum1], *acts)
    hidden1, dact1, *grads = acts
    sum2 = Chain(scatter_chain(grads, n))
    dx1, datt, datt_t = mlp_back1(x1, crel, gain_m, dn2, dact1, chain3.value)
    dx1, datt, datt_t = window([sum1, sum2], [sum1, sum2], dx1, datt, datt_t)

    tables = (cos, sin, qg, kg)
    per = KEY_VALUE_HEADS // 4

    def heads(i, before, grads):
        return attend_back(
            datt, n1_t, w_in, q, k, v, rawq, rawk, lse, first, tables,
            i * per, per, before, grads,
        )

    gain0, *rest = heads(0, None, out_grad(datt_t, o))
    gain0, *rest = window([sum2, sum1], [sum1, sum2], gain0, *rest)
    gain1, *rest = heads(1, rest[2:], rest[:2])
    gain1, *rest = window([sum2, sum1], [sum2, sum1], gain1, *rest)
    sum3 = Chain(scatter_chain(rest[:2], n, split=False))
    gain2, *rest = heads(2, rest[2:], None)
    gain2, *rest = window([sum2, sum3], [sum2, sum3], gain2, *rest)
    gain3, *rest = heads(3, rest[2:], rest[:2])
    gain3, res, *rest = window([sum2, sum3], [sum2, sum3], gain3, res, *rest)
    sum4 = Chain(scatter_chain(rest[:2], n, split=False))
    dq, dk, dv = rest[2:]
    result = make_result(res, perm, hidden1, chain3.value)
    result, dq, dk, dv = window([sum4, sum3], [sum4, sum3], result, dq, dk, dv)
    total = Chain(sum_chain((gain0 + gain1) + (gain2 + gain3), n))
    last = [sum4, sum3, total]
    grad_tokens = input_back(trel, dx1, gain_a, perm, dq, dk, dv, w_in)
    (grad_tokens,) = window(last, last, grad_tokens)
    finish(sum1, sum2)
    grad_down, grad_gate, grad_up, grad_mlp_gain = mlp_total(
        mlp_gain, w_gate, w_up, sum1.value, sum2.value
    )
    (grad_mlp_gain,) = window(last, last, grad_mlp_gain)
    finish(*last)
    grad_out, grad_query, grad_key, grad_value, grad_attn_gain = attn_total(
        attn_gain, w_query, w_key, w_value, sum3.value, sum4.value
    )
    return (
        result,
        grad_tokens,
        grad_query,
        grad_key,
        grad_value,
        grad_out.T,
        grad_gate,
        grad_up,
        grad_down.T,
        grad_attn_gain[:, 0],
        grad_mlp_gain[:, 0],
        total.value[0],
        total.value[1],
    )


def solution(mesh):
    n = mesh.shape[AX]
    rows, cols, one = P(AX, None), P(None, AX), P(AX)
    in_specs = (rows, rows, rows, rows, rows, rows, cols, rows, rows, cols, one, one, P(), P())
    out_specs = (rows, rows, rows, rows, rows, cols, rows, rows, cols, one, one, P(), P())
    return jax.shard_map(
        functools.partial(per_device, n), mesh=mesh, in_specs=in_specs, out_specs=out_specs, check_vma=False
    )
```

```python
import functools
import math

import jax
import jax.numpy as jnp
from jax import lax
from jax.experimental import pallas as pl
from jax.experimental.pallas import tpu as pltpu
from jax.sharding import PartitionSpec as P

AX = "fsdp"
D = 1024
HALF = D // 2
QUERY_HEADS = 16
KEY_VALUE_HEADS = 8
HEAD_SIZE = 128
FF = 3072
PART = FF // 2
GROUP = QUERY_HEADS // KEY_VALUE_HEADS
QW = QUERY_HEADS * HEAD_SIZE
KW = KEY_VALUE_HEADS * HEAD_SIZE
LONGEST = 512
BLK = 256
BACK_BLK = 128
COLS = 512
STEP = 256
MLP_COLS = 3 * PART
PAIR = GROUP * HEAD_SIZE
EPS = 1e-06
THETA = 1000000.0
ROOT = math.sqrt(HEAD_SIZE)
SCALE2 = math.log2(math.e) / ROOT
VMEM = 56 * 1024 * 1024
F32 = jnp.float32
B16 = jnp.bfloat16


def axes_of(n):
    out, stride = [(1, 2)], 2
    for radix in (2, 2, 4, 4, 4, 4):
        if stride * radix <= n:
            out.append((stride, radix))
            stride *= radix
    while stride < n:
        out.append((stride, 2))
        stride *= 2
    return out


def move(value, n, axis, k):
    s, r = axis
    pairs = [(i, i + ((i // s % r + k) % r - i // s % r) * s) for i in range(n)]
    return lax.ppermute(value, AX, pairs)


def spread(values, n, axis, sign, split):
    places = list(range(1, len(values)))
    stages = [[k for k in places if k % 2 == 0], [k for k in places if k % 2]]
    got = {}
    for stage in stages if split and stages[0] else [places]:
        got.update(zip(stage, (yield [move(values[k], n, axis, sign * k) for k in stage])))
    return [got[k] for k in places]


def gather_chain(value, n, ends_first=True, ring=True):
    ax = axes_of(n)[1:]
    m = len(ax)
    rows, cols = value.shape
    h = rows // 2
    cur = value.reshape((1,) * m + (rows, cols))
    if ends_first:
        for a in range(2, m):
            if ring:
                got = [cur]
                for _ in range(ax[a][1] - 1):
                    got += yield [move(got[-1], n, ax[a], -1)]
            else:
                got = [cur] + (yield from spread([None] + [cur] * (ax[a][1] - 1), n, ax[a], -1, True))
            cur = jnp.concatenate(got, axis=a)
    parts = [cur[..., :h, :], cur[..., h:, :]]
    for pair in ((0, 1), (1, 0)):
        s = yield [move(u, n, ax[a], -1) for u, a in zip(parts, pair)]
        parts = [jnp.concatenate([u, w], axis=a) for u, w, a in zip(parts, s, pair)]
    cur = jnp.stack(parts)
    if not ends_first:
        for a in range(2, m):
            got = [cur]
            for _ in range(ax[a][1] - 1):
                got += yield [move(got[-1], n, ax[a], -1)]
            cur = jnp.concatenate(got, axis=a + 1)
    cur = cur.reshape(rows * n // 2, cols)
    s = yield [move(cur, n, (1, 2), 1)]
    return [cur] + s


def scatter_chain(blocks, n, split=True):
    ax = axes_of(n)[1:]
    cols = blocks[0].shape[1]
    h = D // n // 2
    keep, give = blocks
    (s,) = yield [move(give, n, (1, 2), 1)]
    acc = (keep.astype(F32) + s.astype(F32)).astype(B16)
    acc = acc.reshape((2,) + tuple(r for _, r in ax) + (h, cols))
    parts = [acc[0], acc[1]]

    def part(u, j, a):
        return lax.index_in_dim(u, j, a, keepdims=True)

    for pair in ((0, 1), (1, 0)):
        s = yield [move(part(u, 1, a), n, ax[a], 1) for u, a in zip(parts, pair)]
        parts = [
            (part(u, 0, a).astype(F32) + w.astype(F32)).astype(B16) for u, w, a in zip(parts, s, pair)
        ]
    acc = jnp.stack(parts)
    for a in range(len(ax) - 1, 1, -1):
        r = ax[a][1]
        s = yield from spread([part(acc, k, a + 1) for k in range(r)], n, ax[a], 1, split)
        terms = [part(acc, 0, a + 1)] + s
        acc = sum(u.astype(F32) for u in terms).astype(B16)
    return [u.reshape(2 * h, cols) for u in terms]


class Chain:
    def __init__(self, steps, stages=0):
        self.steps, self.sent, self.value, self.stages = steps, None, None, stages

    def start(self):
        if self.value is not None:
            return
        try:
            self.sent = self.steps.send(self.sent)
            self.stages -= 1
        except StopIteration as end:
            self.sent, self.value = None, end.value


def window(start, wait, *values):
    for c in start:
        c.start()
    live = [c for c in wait if c.sent is not None]
    if not live:
        return values
    sent, values = lax.optimization_barrier(([c.sent for c in live], values))
    for c, u in zip(live, sent):
        c.sent = u
    return values


def finish(*chains):
    while any(c.value is None for c in chains):
        left = [c for c in chains if c.value is None]
        window(left, left)


def absolute_rows(n):
    ax = axes_of(n)
    me = lax.axis_index(AX)
    share = D // n
    h = share // 2
    place = lax.broadcasted_iota(jnp.int32, (D,), 0)
    inner = place % h
    rem = place // h
    owner = jnp.zeros_like(place)
    for s, r in ax[:0:-1]:
        owner = owner + ((me // s + rem % r) % r) * s
        rem = rem // r
    owner = owner + (me + rem // 2) % 2
    return owner * share + (rem % 2) * h + inner


def sum_chain(value, n):
    step = 1
    while step < n:
        masks = (1, 2, 3) if 4 * step <= n else (1,)
        got = yield [lax.ppermute(value, AX, [(i, i ^ (m * step)) for i in range(n)]) for m in masks]
        value = value + got[0]
        if len(got) > 1:
            value = value + (got[1] + got[2])
        step *= len(masks) + 1
    return value


def call(kernel, grid, ins, outs, shapes, scratch=(), flops=0, moved=0, name=None):
    return pl.pallas_call(
        kernel,
        grid=grid,
        in_specs=ins,
        out_specs=outs,
        out_shape=shapes,
        scratch_shapes=list(scratch),
        compiler_params=pltpu.CompilerParams(vmem_limit_bytes=VMEM),
        cost_estimate=pl.CostEstimate(flops=flops, bytes_accessed=moved, transcendentals=0),
        name=name,
    )


def whole(shape):
    return pl.BlockSpec(shape, lambda *_: (0,) * len(shape))


def rows_of(cols, blk=BLK):
    return pl.BlockSpec((blk, cols), lambda i: (i, 0))


def sds(shape, dtype):
    return jax.ShapeDtypeStruct(shape, dtype)


def nn(a, b):
    return lax.dot_general(a, b, (((1,), (0,)), ((), ())), preferred_element_type=F32)


def nt(a, b):
    return lax.dot_general(a, b, (((1,), (1,)), ((), ())), preferred_element_type=F32)


def inv_rms(x):
    return lax.rsqrt(jnp.mean(x * x, axis=-1, keepdims=True) + EPS)


def chained(kernel, grid, ins, args, outs, shapes, before, scratch=(), flops=0, moved=0, name=None):
    if before is None or isinstance(before, dict):
        before = before or {}
    else:
        before = dict(enumerate(before))
    extra = list(before.values())
    n_in, n_extra = len(ins), len(extra)

    def body(*refs):
        kernel(*refs[:n_in], *refs[n_in + n_extra :])

    return pl.pallas_call(
        body,
        grid=grid,
        in_specs=list(ins) + [pl.BlockSpec(memory_space=pl.ANY)] * n_extra,
        out_specs=outs,
        out_shape=shapes,
        scratch_shapes=list(scratch),
        input_output_aliases={n_in + i: place for i, place in enumerate(before)},
        compiler_params=pltpu.CompilerParams(vmem_limit_bytes=VMEM),
        cost_estimate=pl.CostEstimate(flops=flops, bytes_accessed=moved, transcendentals=0),
        name=name,
    )(*args, *extra)


def halves_of(cols, where):
    return [pl.BlockSpec((HALF, cols), lambda j: (0, where(j)))] * 2


def joined(refs):
    return jnp.concatenate([r[...] for r in refs], axis=0)


def chunks(t, blk=BLK):
    return [slice(i * blk, (i + 1) * blk) for i in range(t // blk)]


def prep_kernel(tok, cot, perm, trel, crel, crel_t):
    trel[...] = nn(tok[...], perm[...]).astype(B16)
    c = nn(cot[...], perm[...]).astype(B16)
    crel[...] = c
    crel_t[...] = c.T


def prep(tokens, cotangent, perm):
    t = tokens.shape[0]
    return call(
        prep_kernel,
        (t // BLK,),
        [rows_of(D), rows_of(D), whole((D, D))],
        [rows_of(D), rows_of(D), pl.BlockSpec((D, BLK), lambda i: (0, i))],
        [sds((t, D), B16), sds((t, D), B16), sds((D, t), B16)],
        flops=4 * t * D * D,
        moved=12 * t * D,
        name="prep",
    )(tokens, cotangent, perm)


def head_rows(n1, w, cos, sin, gain, out, raw):
    for at in chunks(n1.shape[0]):
        x = nn(n1[at, :], w)
        raw[at, :] = x.astype(B16)
        for h in range(COLS // HEAD_SIZE):
            lanes = slice(h * HEAD_SIZE, (h + 1) * HEAD_SIZE)
            y = x[:, lanes]
            y = y * inv_rms(y) * gain[...]
            y = y * cos[at, :] + pltpu.roll(y, HEAD_SIZE // 2, 1) * sin[at, :]
            out[at, lanes] = y.astype(B16)


def queries_kernel(trel, g0, g1, w0, w1, cos, sin, qg, q, rawq, n1, n1_t, gains):
    @pl.when(pl.program_id(0) == 0)
    def _():
        gains[...] = joined((g0, g1)).astype(F32).T[:8]
        gain = gains[0:1, :]
        for at in chunks(trel.shape[0]):
            x = trel[at, :].astype(F32)
            x = (x * inv_rms(x) * gain).astype(B16)
            n1[at, :] = x
            n1_t[:, at] = x.T

    head_rows(n1, joined((w0, w1)), cos, sin, qg, q, rawq)


def project_queries(trel, w, cos, sin, qg):
    t = trel.shape[0]
    table, one = whole((t, HEAD_SIZE)), whole((1, HEAD_SIZE))
    out = pl.BlockSpec((t, COLS), lambda j: (0, j))
    return call(
        queries_kernel,
        (QW // COLS,),
        [whole((t, D))] + halves_of(HEAD_SIZE, lambda j: 3 * QW // HEAD_SIZE)
        + halves_of(COLS, lambda j: j) + [table, table, one],
        [out, out, whole((t, D)), whole((D, t)), whole((8, D))],
        [sds((t, QW), B16)] * 2 + [sds((t, D), B16), sds((D, t), B16), sds((8, D), F32)],
        flops=2 * t * D * QW,
        moved=2 * (D * QW + t * (2 * QW + 3 * D)),
        name="project_queries",
    )(trel, *w, *w, cos, sin, qg)


def keys_kernel(n1, w0, w1, cos, sin, kg, k, rawk, v):
    w = joined((w0, w1))

    @pl.when(pl.program_id(0) < KW // COLS)
    def _():
        head_rows(n1, w, cos, sin, kg, k, rawk)

    @pl.when(pl.program_id(0) >= KW // COLS)
    def _():
        for at in chunks(n1.shape[0]):
            v[at, :] = nn(n1[at, :], w).astype(B16)


def project_keys(n1, w, cos, sin, kg):
    t = n1.shape[0]
    nk = KW // COLS
    table, one = whole((t, HEAD_SIZE)), whole((1, HEAD_SIZE))
    early = pl.BlockSpec((t, COLS), lambda j: (0, jnp.minimum(j, nk - 1)))
    late = pl.BlockSpec((t, COLS), lambda j: (0, jnp.maximum(j - nk, 0)))
    return call(
        keys_kernel,
        (2 * nk,),
        [whole((t, D))] + halves_of(COLS, lambda j: QW // COLS + j) + [table, table, one],
        [early, early, late],
        [sds((t, KW), B16)] * 3,
        flops=4 * t * D * KW,
        moved=2 * (2 * D * KW + t * (3 * KW + D)),
        name="project_keys",
    )(n1, *w, cos, sin, kg)


def build_bias(first, bias):
    t = bias.shape[0]
    for i, at in enumerate(chunks(t)):
        key = lax.broadcasted_iota(jnp.int32, (t, BLK), 0)
        query = lax.broadcasted_iota(jnp.int32, (t, BLK), 1) + i * BLK
        allowed = (key >= first[:, at]) & (key <= query)
        bias[:, at] = jnp.where(allowed, 0.0, -1e30)


def window_of(i, blk=BLK):
    return slice(max(0, i - LONGEST // blk) * blk, (i + 1) * blk)


def stacked(ref, at):
    return jnp.concatenate([ref[at, :HEAD_SIZE], ref[at, HEAD_SIZE:]], axis=0)


def attend_kernel(q, k, v, first, out, lse, bias):
    @pl.when(pl.program_id(0) == 0)
    def _():
        build_bias(first, bias)

    vt = v[...].T
    for i, at in enumerate(chunks(q.shape[0])):
        keys = window_of(i)
        s = nt(k[keys, :], stacked(q, at))
        b = bias[keys, at]
        e = jnp.exp2(s * SCALE2 + jnp.concatenate([b, b], axis=1))
        total = jnp.sum(e, axis=0, keepdims=True)
        o = (nn(vt[:, keys], e.astype(B16)) * (1.0 / total)).T.astype(B16)
        level = jnp.log2(total)
        for r in range(GROUP):
            mine = slice(r * BLK, (r + 1) * BLK)
            out[at, r * HEAD_SIZE : (r + 1) * HEAD_SIZE] = o[mine, :]
            lse[0, r : r + 1, at] = level[:, mine]


def attend(q, k, v, first):
    t = k.shape[0]
    groups = k.shape[1] // HEAD_SIZE
    head = pl.BlockSpec((t, HEAD_SIZE), lambda g: (0, g))
    both = pl.BlockSpec((t, PAIR), lambda g: (0, g))
    return call(
        attend_kernel,
        (groups,),
        [both, head, head, whole((1, t))],
        [both, pl.BlockSpec((1, GROUP, t), lambda g: (g, 0, 0))],
        [sds((t, groups * PAIR), B16), sds((groups, GROUP, t), F32)],
        [pltpu.VMEM((t, t), F32)],
        flops=8 * groups * t * t * PAIR,
        moved=12 * t * groups * HEAD_SIZE,
        name="attend",
    )(q, k, v, first)


def after_kernel(o, *refs):
    *w, trel, gain, x1, n2, n2_t = refs
    x = trel[...].astype(F32)
    for i in range(len(w) // 2):
        part = o[:, i * COLS : (i + 1) * COLS]
        x = x + nt(part, joined(w[2 * i : 2 * i + 2]))
    x1[...] = x
    y = (x * inv_rms(x) * gain[...]).astype(B16)
    n2[...] = y
    n2_t[...] = y.T


def after_attention(o, w, trel, gain):
    t = o.shape[0]
    count = QW // COLS
    specs = [halves_of(COLS, lambda i, c=c: 2 * QW // COLS + c) for c in range(count)]
    return call(
        after_kernel,
        (t // BLK,),
        [rows_of(QW)] + [u for pair in specs for u in pair] + [rows_of(D), whole((1, D))],
        [rows_of(D), rows_of(D), pl.BlockSpec((D, BLK), lambda i: (0, i))],
        [sds((t, D), F32), sds((t, D), B16), sds((D, t), B16)],
        flops=2 * t * D * QW,
        moved=2 * (t * QW + D * QW + 5 * t * D),
        name="after_attention",
    )(o, *(list(w) * count), trel, gain)


def mlp_kernel(n2, n2_t, c, c_t, w0, w1, hidden, dact, g0, g1):
    w = joined((w0, w1))
    for at in chunks(n2.shape[0]):
        x = nn(n2[at, :], w[:, STEP:])
        gate, up = x[:, :STEP], x[:, STEP:]
        dh = nn(c[at, :], w[:, :STEP])
        sig = jax.nn.sigmoid(gate)
        silu = gate * sig
        hidden[at, :] = (silu * up).astype(B16)
        dact[at, :STEP] = (dh * up * sig * (1.0 + gate * (1.0 - sig))).astype(B16)
        dact[at, STEP:] = (dh * silu).astype(B16)
    for p, out in enumerate((g0, g1)):
        mine = slice(p * HALF, (p + 1) * HALF)
        out[:, :STEP] = nn(c_t[mine, :], hidden[...]).astype(B16)
        out[:, STEP:] = nn(n2_t[mine, :], dact[...]).astype(B16)


def mlp(n2, n2_t, c, c_t, w, base, steps, cols, before):
    t = n2.shape[0]

    def at(width):
        return pl.BlockSpec((t, width), lambda j: (0, base + j))

    return chained(
        mlp_kernel,
        (steps,),
        [whole((t, D)), whole((D, t))] * 2 + halves_of(3 * STEP, lambda j: base + j),
        [n2, n2_t, c, c_t, *w],
        [at(STEP), at(2 * STEP)] + halves_of(3 * STEP, lambda j: base + j),
        [sds((t, PART), B16), sds((t, 2 * PART), B16)] + [sds((HALF, cols), B16)] * 2,
        before,
        flops=12 * t * D * STEP * steps,
        moved=8 * t * D + steps * STEP * (12 * D + 6 * t),
        name="mlp",
    )


def mlp_back0_kernel(x1, hidden, dact, w0, w1, dn2, res):
    @pl.when(pl.program_id(0) == 0)
    def _():
        dn2[...] = jnp.zeros_like(dn2)
        res[...] = x1[...]

    w = joined((w0, w1))
    for at in chunks(x1.shape[0]):
        dn2[at, :] += nt(dact[at, :], w[:, STEP:])
        res[at, :] += nt(hidden[at, :], w[:, :STEP])


def mlp_back0(x1, hidden, dact, w):
    t = x1.shape[0]

    def at(width):
        return pl.BlockSpec((t, width), lambda j: (0, j))

    return call(
        mlp_back0_kernel,
        (PART // STEP,),
        [whole((t, D)), at(STEP), at(2 * STEP)] + halves_of(3 * STEP, lambda j: j),
        [whole((t, D)), whole((t, D))],
        [sds((t, D), F32)] * 2,
        flops=6 * t * D * PART,
        moved=12 * t * D + 6 * PART * (t + D),
        name="mlp_back0",
    )(x1, hidden, dact, *w)


def mlp_back1_kernel(
    x1_in, crel_in, dn2_in, gain, dact, w0, w1, dx1, datt, datt_t, x1, crel, dn2, sems
):
    j = pl.program_id(0)
    loads = [
        pltpu.make_async_copy(src, dst, sems.at[i])
        for i, (src, dst) in enumerate(((x1_in, x1), (crel_in, crel), (dn2_in, dn2)))
    ]

    @pl.when(j == 0)
    def _():
        for c in loads:
            c.start()
        dx1[...] = jnp.zeros_like(dx1)

    w = joined((w0, w1))[:, STEP:]
    for at in chunks(dx1.shape[0]):
        dx1[at, :] += nt(dact[at, :], w)

    @pl.when(j == pl.num_programs(0) - 1)
    def _():
        for c in loads:
            c.wait()
        for at in chunks(dx1.shape[0]):
            x = x1[at, :]
            s = inv_rms(x)
            r = x * s
            grad = (dx1[at, :] + dn2[at, :]) * gain[...]
            inner = jnp.mean(grad * r, axis=-1, keepdims=True)
            d = crel[at, :].astype(F32) + s * (grad - r * inner)
            dx1[at, :] = d
            low = d.astype(B16)
            datt[at, :] = low
            datt_t[:, at] = low.T


def mlp_back1(x1, crel, gain, dn2, dact, w):
    t = x1.shape[0]
    return call(
        mlp_back1_kernel,
        (PART // STEP,),
        [pl.BlockSpec(memory_space=pl.ANY)] * 3
        + [whole((1, D)), pl.BlockSpec((t, 2 * STEP), lambda j: (0, j))]
        + halves_of(3 * STEP, lambda j: j),
        [whole((t, D)), whole((t, D)), whole((D, t))],
        [sds((t, D), F32), sds((t, D), B16), sds((D, t), B16)],
        [pltpu.VMEM((t, D), F32), pltpu.VMEM((t, D), B16), pltpu.VMEM((t, D), F32),
         pltpu.SemaphoreType.DMA((3,))],
        flops=4 * t * D * PART,
        moved=18 * t * D + 4 * PART * (t + D),
        name="mlp_back1",
    )(x1, crel, dn2, gain, dact, *w)


def out_grad_kernel(datt_t, o, g0, g1):
    for p, out in enumerate((g0, g1)):
        out[...] = nn(datt_t[p * HALF : (p + 1) * HALF, :], o[...]).astype(B16)


def out_grad(datt_t, o):
    t = o.shape[0]
    return chained(
        out_grad_kernel,
        (QW // COLS,),
        [whole((D, t)), pl.BlockSpec((t, COLS), lambda j: (0, j))],
        [datt_t, o],
        halves_of(COLS, lambda j: j),
        [sds((HALF, 2 * QW), B16)] * 2,
        None,
        flops=2 * t * D * QW,
        moved=2 * (t * D + t * QW + D * QW),
        name="out_grad",
    )


def result_kernel(res, perm, hidden, w0, w1, out, acc):
    j = pl.program_id(0)

    @pl.when(j == 0)
    def _():
        acc[...] = res[...]

    w = joined((w0, w1))
    for at in chunks(res.shape[0]):
        acc[at, :] += nt(hidden[at, :], w)

    @pl.when(j == pl.num_programs(0) - 1)
    def _():
        for at in chunks(res.shape[0]):
            out[at, :] = nt(acc[at, :].astype(B16), perm[...]).astype(B16)


def make_result(res, perm, hidden, w):
    t = res.shape[0]
    return call(
        result_kernel,
        (PART // STEP,),
        [whole((t, D)), whole((D, D)), pl.BlockSpec((t, STEP), lambda j: (0, j))]
        + halves_of(STEP, lambda j: 3 * j),
        whole((t, D)),
        sds((t, D), B16),
        [pltpu.VMEM((t, D), F32)],
        flops=2 * t * D * (PART + D),
        moved=2 * (t * PART + D * PART + 3 * t * D + D * D),
        name="result",
    )(res, perm, hidden, *w)


def head_back(dy, raw, cos, sin, gain):
    dn = dy * cos - pltpu.roll(dy, HEAD_SIZE // 2, 1) * sin
    x = raw.astype(F32)
    s = inv_rms(x)
    r = x * s
    grad = dn * gain
    inner = jnp.mean(grad * r, axis=-1, keepdims=True)
    return (s * (grad - r * inner)).astype(B16), jnp.sum(dn * r, axis=0, keepdims=True)


def attend_back_kernel(
    datt, n1_t, w0, w1, q, k, v, rawq, rawk, lse, first, cos, sin, qgain, kgain,
    gains, g0, g1, dq, dk, dv, bias, do, dk_sum, dv_sum, low,
):
    @pl.when(pl.program_id(0) == 0)
    def _():
        build_bias(first, bias)
        gains[...] = jnp.zeros_like(gains)

    t = q.shape[0]
    w = joined((w0, w1))
    for at in chunks(t):
        do[at, :] = nn(datt[at, :], w).astype(B16)
    kt = k[...].T
    dk_sum[...] = jnp.zeros_like(dk_sum)
    dv_sum[...] = jnp.zeros_like(dv_sum)
    for i, at in enumerate(chunks(t, BACK_BLK)):
        keys = window_of(i, BACK_BLK)
        q2, do2 = stacked(q, at), stacked(do, at)
        b = bias[keys, at]
        level = jnp.concatenate([lse[0, r : r + 1, at] for r in range(GROUP)], axis=1)
        s = nt(k[keys, :], q2)
        p = jnp.exp2(s * SCALE2 + jnp.concatenate([b, b], axis=1) - level)
        dp = nt(v[keys, :], do2)
        delta = jnp.sum(dp * p, axis=0, keepdims=True)
        ds = (p * (dp - delta)).astype(B16)
        dv_sum[keys, :] += nn(p.astype(B16), do2)
        dk_sum[keys, :] += nn(ds, q2)
        dq2 = nn(kt[:, keys], ds).T * (1.0 / ROOT)
        for r in range(GROUP):
            lanes = slice(r * HEAD_SIZE, (r + 1) * HEAD_SIZE)
            grad, part = head_back(
                dq2[r * BACK_BLK : (r + 1) * BACK_BLK, :], rawq[at, lanes], cos[at, :], sin[at, :], qgain[...]
            )
            low[at, lanes] = grad
            gains[0:1, :] += part
    for at in chunks(t):
        grad, part = head_back(
            dk_sum[at, :] * (1.0 / ROOT), rawk[at, :], cos[at, :], sin[at, :], kgain[...]
        )
        low[at, PAIR : PAIR + HEAD_SIZE] = grad
        gains[1:2, :] += part
    low[:, PAIR + HEAD_SIZE :] = dv_sum[...].astype(B16)
    dq[...] = low[:, :PAIR]
    dk[...] = low[:, PAIR : PAIR + HEAD_SIZE]
    dv[...] = low[:, PAIR + HEAD_SIZE :]
    for p, out in enumerate((g0, g1)):
        out[...] = nn(n1_t[p * HALF : (p + 1) * HALF, :], low[...]).astype(B16)


def attend_back(datt, n1_t, w, q, k, v, rawq, rawk, lse, first, tables, base, count, before, grads):
    t = k.shape[0]
    groups = k.shape[1] // HEAD_SIZE
    per = groups // 2
    ahead = QW // (2 * PAIR) if base < per else 0
    head = pl.BlockSpec((t, HEAD_SIZE), lambda g: (0, base + g))
    both = pl.BlockSpec((t, PAIR), lambda g: (0, base + g))
    table, one = whole((t, HEAD_SIZE)), whole((1, HEAD_SIZE))
    shapes = [sds((8, HEAD_SIZE), F32)] + [sds((HALF, (ahead + per) * 2 * PAIR), B16)] * 2
    shapes += [sds((t, QW), B16), sds((t, KW), B16), sds((t, KW), B16)]
    earlier = {1 + i: u for i, u in enumerate(grads or ())}
    earlier.update({3 + i: u for i, u in enumerate(before or ())})
    return chained(
        attend_back_kernel,
        (count,),
        [whole((t, D)), whole((D, t))] + halves_of(PAIR, lambda g: 2 * QW // PAIR + base + g)
        + [both, head, head, both, head, pl.BlockSpec((1, GROUP, t), lambda g: (base + g, 0, 0)),
           whole((1, t)), table, table, one, one],
        [datt, n1_t, *w, q, k, v, rawq, rawk, lse, first, *tables],
        [whole((8, HEAD_SIZE))] + halves_of(2 * PAIR, lambda g: ahead + (base + g) % per) + [both, head, head],
        shapes,
        earlier,
        [pltpu.VMEM((t, t), F32), pltpu.VMEM((t, PAIR), B16), pltpu.VMEM((t, HEAD_SIZE), F32),
         pltpu.VMEM((t, HEAD_SIZE), F32), pltpu.VMEM((t, 2 * PAIR), B16)],
        flops=count * (6 * t * D * PAIR + 10 * t * t * PAIR),
        moved=4 * t * D + count * (12 * t * HEAD_SIZE * 2 + 6 * D * PAIR),
        name="attend_back",
    )


def input_back_kernel(trel, dx1, gain, perm, dq, dk, dv, w0, w1, out):
    grad = jnp.concatenate(
        [
            nt(dq[...], w[:, :QW]) + nt(dk[...], w[:, QW : QW + KW]) + nt(dv[...], w[:, QW + KW :])
            for w in (w0, w1)
        ],
        axis=1,
    )
    x = trel[...].astype(F32)
    s = inv_rms(x)
    r = x * s
    grad = grad * gain[...]
    inner = jnp.mean(grad * r, axis=-1, keepdims=True)
    d = (dx1[...] + s * (grad - r * inner)).astype(B16)
    out[...] = nt(d, perm[...]).astype(B16)


def input_back(trel, dx1, gain, perm, dq, dk, dv, w):
    t = trel.shape[0]
    return call(
        input_back_kernel,
        (t // BLK,),
        [rows_of(D), rows_of(D), whole((1, D)), whole((D, D)), rows_of(QW), rows_of(KW), rows_of(KW)]
        + halves_of(QW + 2 * KW, lambda i: 0),
        rows_of(D),
        sds((t, D), B16),
        flops=2 * t * D * (QW + 2 * KW + D),
        moved=2 * (t * (QW + 2 * KW) + D * (QW + 2 * KW) + 4 * t * D + D * D),
        name="input_back",
    )(trel, dx1, gain, perm, dq, dk, dv, *w)


def added(refs, cols):
    return functools.reduce(lambda u, w: u + w, [r[:, cols].astype(F32) for r in refs])


def mlp_total_kernel(count, gain, wg, wu, *refs):
    sums, (down, gate, up, grad_gain) = (refs[:count], refs[count : 2 * count]), refs[2 * count :]
    total = jnp.zeros(grad_gain.shape, F32)
    for i, terms in enumerate(sums):
        for j in range(PART // STEP):
            x = added(terms, slice(3 * j * STEP, 3 * (j + 1) * STEP))
            at = slice(i * PART + j * STEP, i * PART + (j + 1) * STEP)
            down[:, at] = x[:, :STEP]
            gate[:, at] = x[:, STEP : 2 * STEP]
            up[:, at] = x[:, 2 * STEP :]
            both = wg[:, at].astype(F32) * x[:, STEP : 2 * STEP] + wu[:, at].astype(F32) * x[:, 2 * STEP :]
            total = total + jnp.sum(both, axis=1, keepdims=True)
    grad_gain[...] = total / gain[...].astype(F32)


def mlp_total(gain, wg, wu, first, second):
    share = wg.shape[0]
    ins = [gain.reshape(share, 1), wg, wu, *first, *second]
    shapes = [sds((share, FF), F32)] * 3 + [sds((share, 1), F32)]
    return call(
        functools.partial(mlp_total_kernel, len(first)),
        (1,),
        [whole(u.shape) for u in ins],
        [whole(u.shape) for u in shapes],
        shapes,
        moved=share * FF * 40,
        name="mlp_total",
    )(*ins)


def attn_total_kernel(count, gain, wq, wk, wv, *refs):
    early, late = refs[:count], refs[count : 2 * count]
    out, q, k, v, grad_gain = refs[2 * count :]
    out[...] = added(early, slice(0, QW))
    total = jnp.zeros(grad_gain.shape, F32)
    half = KEY_VALUE_HEADS // 2
    for g in range(KEY_VALUE_HEADS):
        terms, start = (early, QW + 2 * PAIR * g) if g < half else (late, 2 * PAIR * (g - half))
        x = added(terms, slice(start, start + 2 * PAIR))
        wide, head = slice(g * PAIR, (g + 1) * PAIR), slice(g * HEAD_SIZE, (g + 1) * HEAD_SIZE)
        q[:, wide] = x[:, :PAIR]
        k[:, head] = x[:, PAIR : PAIR + HEAD_SIZE]
        v[:, head] = x[:, PAIR + HEAD_SIZE :]
        w = jnp.concatenate([wq[:, wide], wk[:, head], wv[:, head]], axis=1)
        total = total + jnp.sum(w.astype(F32) * x, axis=1, keepdims=True)
    grad_gain[...] = total / gain[...].astype(F32)


def attn_total(gain, wq, wk, wv, early, late):
    share = wq.shape[0]
    ins = [gain.reshape(share, 1), wq, wk, wv, *early, *late]
    shapes = [sds((share, QW), F32)] * 2 + [sds((share, KW), F32)] * 2 + [sds((share, 1), F32)]
    return call(
        functools.partial(attn_total_kernel, len(early)),
        (1,),
        [whole(u.shape) for u in ins],
        [whole(u.shape) for u in shapes],
        shapes,
        moved=share * (QW + KW) * 40,
        name="attn_total",
    )(*ins)


def run_starts(segment_row):
    index = jnp.arange(segment_row.shape[0], dtype=jnp.int32)
    previous = jnp.concatenate([segment_row[:1] - 1, segment_row[:-1]])
    return index, lax.cummax(jnp.where(segment_row != previous, index, 0), axis=0)


def by_step(gate, up, down):
    rows = gate.shape[0]
    three = [w.reshape(rows, -1, 1, STEP) for w in (down, gate, up)]
    return jnp.concatenate(three, axis=2).reshape(rows, -1)


def per_device(
    n, tokens, segments, cotangent, w_query, w_key, w_value, w_out, w_gate, w_up, w_down,
    attn_gain, mlp_gain, q_gain, k_gain,
):
    share = D // n
    steps = PART // STEP
    count = len(axes_of(n))
    gain_cols = jnp.concatenate([attn_gain[:, None], mlp_gain[:, None]], axis=1)
    gain_cols = jnp.pad(gain_cols, ((0, 0), (0, HEAD_SIZE - 2)))
    down_t = w_down.T
    halves = [
        by_step(w_gate[:, cols], w_up[:, cols], down_t[:, cols])
        for cols in (slice(0, PART), slice(PART, FF))
    ]
    shards1 = jnp.concatenate([w_query, w_key, w_value, w_out.T, gain_cols], axis=1)
    ends = [r for _, r in axes_of(n)[3:]]
    chain1 = Chain(gather_chain(shards1, n), 3 + sum(r - 1 for r in ends))
    chain2 = Chain(gather_chain(halves[0], n, ring=False), 3 + sum(1 + (r > 2) for r in ends))
    chain3 = Chain(gather_chain(halves[1], n, ends_first=False), 3 + sum(r - 1 for r in ends))

    index, first = run_starts(segments[0])
    half = HEAD_SIZE // 2
    freq = THETA ** (-jnp.arange(half, dtype=F32) / half)
    turned = (index - first).astype(F32)[:, None] * freq[None, :]
    cos, sin = jnp.cos(turned), jnp.sin(turned)
    cos = jnp.concatenate([cos, cos], axis=1)
    sin = jnp.concatenate([-sin, sin], axis=1)
    first = first.reshape(1, -1)
    qg = q_gain.astype(F32).reshape(1, HEAD_SIZE)
    kg = k_gain.astype(F32).reshape(1, HEAD_SIZE)
    perm = (jnp.arange(D, dtype=jnp.int32)[:, None] == absolute_rows(n)[None, :]).astype(B16)

    window([chain1, chain3], [chain1, chain3])
    cos, sin, perm = window([chain1, chain3], [chain1, chain3], cos, sin, perm)
    while chain1.stages > 3:
        window([chain1], [chain1])
    tokens, cotangent = window([chain1, chain2], [chain1, chain2], tokens, cotangent)
    while chain2.stages > 4:
        window([chain2], [chain2])
    every = [chain1, chain2, chain3]
    trel, crel, crel_t = prep(tokens, cotangent, perm)
    trel, crel, crel_t = window(every, every, trel, crel, crel_t)
    while chain3.stages > 3:
        window([chain3], [chain3])
    window([chain1, chain2], [chain1, chain2])
    finish(chain1)
    w_in = chain1.value

    q, rawq, n1, n1_t, gains = project_queries(trel, w_in, cos, sin, qg)
    gain_a, gain_m = gains[0:1], gains[1:2]
    k, rawk, v = project_keys(n1, w_in, cos, sin, kg)
    q, k, v = window([chain2, chain3], [chain2, chain3], q, k, v)
    o, lse = attend(q, k, v, first)
    o, lse = window([chain2], [chain2], o, lse)
    finish(chain2)
    x1, n2, n2_t = after_attention(o, w_in, trel, gain_m)

    def units(w, base, count, acts):
        return mlp(n2, n2_t, crel, crel_t, w, base, count, MLP_COLS, acts)

    acts = units(chain2.value, 0, steps, None)
    acts = window([chain3], [chain3], *acts)
    hidden0, dact0, *grads = acts
    sum1 = Chain(scatter_chain(grads, n))
    dn2, res = mlp_back0(x1, hidden0, dact0, chain2.value)
    dn2, res = window([chain3, sum1], [chain3, sum1], dn2, res)
    finish(chain3)

    acts = units(chain3.value, 0, steps, None)
    acts = window([sum1], [sum1], *acts)
    hidden1, dact1, *grads = acts
    sum2 = Chain(scatter_chain(grads, n))
    dx1, datt, datt_t = mlp_back1(x1, crel, gain_m, dn2, dact1, chain3.value)
    dx1, datt, datt_t = window([sum1, sum2], [sum1, sum2], dx1, datt, datt_t)

    tables = (cos, sin, qg, kg)
    per = KEY_VALUE_HEADS // 4

    def heads(i, before, grads):
        return attend_back(
            datt, n1_t, w_in, q, k, v, rawq, rawk, lse, first, tables,
            i * per, per, before, grads,
        )

    gain0, *rest = heads(0, None, out_grad(datt_t, o))
    gain0, *rest = window([sum2, sum1], [sum1, sum2], gain0, *rest)
    gain1, *rest = heads(1, rest[2:], rest[:2])
    gain1, *rest = window([sum2, sum1], [sum2, sum1], gain1, *rest)
    sum3 = Chain(scatter_chain(rest[:2], n, split=False))
    gain2, *rest = heads(2, rest[2:], None)
    gain2, *rest = window([sum2, sum3], [sum2, sum3], gain2, *rest)
    gain3, *rest = heads(3, rest[2:], rest[:2])
    gain3, res, *rest = window([sum2, sum3], [sum2, sum3], gain3, res, *rest)
    sum4 = Chain(scatter_chain(rest[:2], n, split=False))
    dq, dk, dv = rest[2:]
    result = make_result(res, perm, hidden1, chain3.value)
    result, dq, dk, dv = window([sum4, sum3], [sum4, sum3], result, dq, dk, dv)
    total = Chain(sum_chain((gain0 + gain1) + (gain2 + gain3), n))
    last = [sum4, sum3, total]
    grad_tokens = input_back(trel, dx1, gain_a, perm, dq, dk, dv, w_in)
    (grad_tokens,) = window(last, last, grad_tokens)
    finish(sum1, sum2)
    grad_down, grad_gate, grad_up, grad_mlp_gain = mlp_total(
        mlp_gain, w_gate, w_up, sum1.value, sum2.value
    )
    (grad_mlp_gain,) = window(last, last, grad_mlp_gain)
    finish(*last)
    grad_out, grad_query, grad_key, grad_value, grad_attn_gain = attn_total(
        attn_gain, w_query, w_key, w_value, sum3.value, sum4.value
    )
    return (
        result,
        grad_tokens,
        grad_query,
        grad_key,
        grad_value,
        grad_out.T,
        grad_gate,
        grad_up,
        grad_down.T,
        grad_attn_gain[:, 0],
        grad_mlp_gain[:, 0],
        total.value[0],
        total.value[1],
    )


def solution(mesh):
    n = mesh.shape[AX]
    rows, cols, one = P(AX, None), P(None, AX), P(AX)
    in_specs = (rows, rows, rows, rows, rows, rows, cols, rows, rows, cols, one, one, P(), P())
    out_specs = (rows, rows, rows, rows, rows, cols, rows, rows, cols, one, one, P(), P())
    return jax.shard_map(
        functools.partial(per_device, n), mesh=mesh, in_specs=in_specs, out_specs=out_specs, check_vma=False
    )
```
